256 devices in a mesh: section: 64 (over y, x, z_hi, core), tensor: 4 (over z_lo).
Axes of the slice: x: 4, y: 4, z: 8 (z_hi: 2, z_lo: 4; z = z_hi * 4 + z_lo), core: 2. Of those that a mesh axis runs over, the one named last changes fastest.
Arguments:
- fwd_in: bfloat16 [64, 256, 2048], P('section', None, 'tensor'), may hold values from -24 to 24
- bwd_in: bfloat16 [64, 256, 2048], P('section', None, 'tensor'), may hold values from -24 to 24
- cotangent: bfloat16 [64, 256, 2048], P('section', None, 'tensor'), may hold values from -6 to 6
- enc_saved: bfloat16 [256, 2048], P(None, 'tensor'), may hold values from -24 to 24
- norm_gain: bfloat16 [64, 2048], P('section', 'tensor'), may hold values from 0.099609375 to 1.8984375
- final_gain: bfloat16 [2048], P('tensor'), may hold values from 0.099609375 to 1.8984375
- w_qkv: bfloat16 [64, 2048, 3, 2048], P('section', None, None, 'tensor'), may hold values from -0.125 to 0.125
- w_out: bfloat16 [64, 2048, 2048], P('section', 'tensor'), may hold values from -0.375 to 0.375
Outputs:
- fwd_out: bfloat16 [64, 256, 2048], P('section', None, 'tensor')
- grad_in: bfloat16 [64, 256, 2048], P('section', None, 'tensor')
The draws below stay inside these ranges and needn't reach their ends.
All inputs are finite; a program needn't handle non-finite values.
Results may differ from the reference program's by a relative error of at most 0.017.
Values may be sent and summed in bfloat16 or wider, within the bound.
No kernel may reach another device: no remote copies, remote signals or barrier semaphores. Data moves between devices by JAX's collectives and lax.ppermute only.
A program may use at most 128 MiB of HBM per device.

```python
import math
import jax
import jax.numpy as jnp
from jax import lax

D = 2048
HEADS = 8
HEAD_DIM = 256
ROWS = 256
SECTIONS = 64
ENC_SECTIONS = 32
N_TENSOR = 4


def scaled(key, fluctuation, lowest, highest, ramp_low, ramp_high):
    row_key, col_key = jax.random.split(key)
    full_shape = fluctuation.shape
    row_scale = jnp.exp(jax.random.uniform(row_key, full_shape[:-1] + (1,), jnp.float32, math.log(lowest), math.log(highest)))
    col_scale = jnp.exp(jax.random.uniform(col_key, full_shape[:-2] + (1, full_shape[-1]), jnp.float32, math.log(0.35), math.log(1.2)))
    position = jnp.arange(full_shape[-1], dtype=jnp.float32) / full_shape[-1]
    feature_ramp = ramp_low * jnp.exp(math.log(ramp_high / ramp_low) * position)
    return jnp.clip(fluctuation * row_scale * col_scale * feature_ramp, -24.0, 24.0).astype(jnp.bfloat16)


def draw_fwd_in(key, part):
    key = jax.random.fold_in(key, 11)
    noise_key = jax.random.fold_in(key, 0)
    scale_key = jax.random.fold_in(key, 2)
    full_shape = (SECTIONS, ROWS, D)
    fluctuation = jax.random.truncated_normal(noise_key, -4.0, 4.0, full_shape, jnp.float32)
    return scaled(scale_key, fluctuation, 0.4, 4.0, 1.0, 3.0)


def draw_bwd_in(key, part):
    key = jax.random.fold_in(key, 23)
    noise_key = jax.random.fold_in(key, 0)
    scale_key = jax.random.fold_in(key, 2)
    full_shape = (SECTIONS, ROWS, D)
    fluctuation = jax.random.truncated_normal(noise_key, -4.0, 4.0, full_shape, jnp.float32)
    return scaled(scale_key, fluctuation, 0.4, 4.0, 0.35, 3.5)


def draw_enc_saved(key, part):
    key = jax.random.fold_in(key, 37)
    noise_key = jax.random.fold_in(key, 0)
    scale_key = jax.random.fold_in(key, 2)
    full_shape = (ROWS, D)
    fluctuation = jax.random.truncated_normal(noise_key, -4.0, 4.0, full_shape, jnp.float32)
    return scaled(scale_key, fluctuation, 0.4, 4.0, 1.0, 3.0)


def level_of(rng, shape, pieces, smallest, high):
    loudness, own = 1.0, jax.random.fold_in(rng, 6)
    for dim, blocks in pieces:
        heights = jnp.exp(jax.random.uniform(jax.random.fold_in(own, dim), (blocks,), jnp.float32, smallest / len(pieces), high / len(pieces)))
        loudness = loudness * jnp.repeat(heights, shape[dim] // blocks).reshape([-1 if axis == dim else 1 for axis in range(len(shape))])
    return loudness


def centred(key, shape, deviation, reach, cuts=(), kind=jnp.bfloat16):
    values = jax.random.normal(key, shape, jnp.float32) * deviation
    if len(cuts) > 0:
        values = level_of(key, shape, cuts, -0.22, 0.18) * values
    return jnp.clip(values, min=-reach, max=reach).astype(kind)


def setup_inputs(seed: int = 0) -> dict:
    arg_keys = jax.random.split(jax.random.key(seed), 9)
    return {
        "fwd_in": draw_fwd_in(jax.random.fold_in(arg_keys[8], 71), 0),
        "bwd_in": draw_bwd_in(jax.random.fold_in(arg_keys[8], 71), 0),
        "cotangent": centred(arg_keys[2], (SECTIONS, ROWS, D), 1.0, 6.0, ((0, 64), (2, 4))),
        "enc_saved": draw_enc_saved(jax.random.fold_in(arg_keys[8], 71), 0),
        "norm_gain": jnp.clip(1.0 + 0.18 * jax.random.normal(arg_keys[4], (SECTIONS, D), jnp.float32), 0.099609375, 1.8984375).astype(jnp.bfloat16),
        "final_gain": jnp.clip(1.0 + 0.18 * jax.random.normal(arg_keys[5], (D,), jnp.float32), 0.099609375, 1.8984375).astype(jnp.bfloat16),
        "w_qkv": centred(arg_keys[6], (SECTIONS, D, 3, HEADS * HEAD_DIM), D ** -0.5, 0.125, ((0, 64), (3, 4))),
        "w_out": centred(arg_keys[7], (SECTIONS, HEADS * HEAD_DIM, D), (HEADS * HEAD_DIM // 8) ** -0.5, 0.375, ((0, 64), (1, 4))),
    }


epsilon = 1e-06

def rounded(values):
    return lax.optimization_barrier(values.astype(jnp.bfloat16))

def inverse_rms(values):
    return lax.rsqrt(lax.optimization_barrier(jnp.mean(values * values, axis=-1, keepdims=True)) + epsilon)

def normalize(values, gain_row):
    return (values * inverse_rms(values) * gain_row.astype(jnp.float32)).astype(jnp.bfloat16)

def split_heads(matrix):
    return matrix.astype(jnp.float32).reshape(matrix.shape[0], HEADS, HEAD_DIM)

def recompute(normed, source, w_qkv):
    queries = rounded(jnp.dot(normed, w_qkv[:, 0], preferred_element_type=jnp.float32))
    key_rows = rounded(jnp.dot(source, w_qkv[:, 1], preferred_element_type=jnp.float32))
    value_rows = rounded(jnp.dot(source, w_qkv[:, 2], preferred_element_type=jnp.float32))
    scores = jnp.einsum('qhd,khd->hqk', split_heads(queries), split_heads(key_rows)) * HEAD_DIM ** (-0.5)
    weights = jnp.exp(scores)
    weights = weights / lax.optimization_barrier(jnp.sum(weights, axis=-1, keepdims=True))
    return (queries, key_rows, value_rows, weights)

def forward(values, gain_row, w_qkv, w_out, source):
    inputs = values.astype(jnp.float32)
    normed = normalize(inputs, gain_row)
    if source is None:
        source = normed
    queries, key_rows, value_rows, weights = recompute(normed, source, w_qkv)
    mixed_rows = rounded(jnp.einsum('hqk,khd->qhd', rounded(weights).astype(jnp.float32), split_heads(value_rows)))
    mixed_rows = mixed_rows.reshape(values.shape[0], HEADS * HEAD_DIM)
    group_width = HEADS * HEAD_DIM // N_TENSOR
    totals = jnp.zeros(inputs.shape, jnp.float32)
    for head_group in range(N_TENSOR):
        columns = slice(head_group * group_width, (head_group + 1) * group_width)
        product = jnp.dot(mixed_rows[:, columns], w_out[columns], preferred_element_type=jnp.float32)
        totals = totals + rounded(product).astype(jnp.float32)
    return (inputs + totals).astype(jnp.bfloat16)

def backward(values, upstream, gain_row, w_qkv, w_out, source):
    row_count = values.shape[0]
    inputs = values.astype(jnp.float32)
    normed = normalize(inputs, gain_row)
    crossing = source is not None
    if not crossing:
        source = normed
    queries, key_rows, value_rows, weights = recompute(normed, source, w_qkv)
    grad_mix = rounded(jnp.dot(upstream, w_out.T, preferred_element_type=jnp.float32))
    grad_heads = split_heads(grad_mix)
    grad_values = rounded(jnp.einsum('hqk,qhd->khd', rounded(weights).astype(jnp.float32), grad_heads))
    grad_values = grad_values.reshape(row_count, HEADS * HEAD_DIM)
    grad_weights = jnp.einsum('qhd,khd->hqk', grad_heads, split_heads(value_rows))
    grad_scores = weights * (grad_weights - lax.optimization_barrier(jnp.sum(weights * grad_weights, axis=-1, keepdims=True))) * HEAD_DIM ** (-0.5)
    grad_scores = rounded(grad_scores).astype(jnp.float32)
    grad_query = rounded(jnp.einsum('hqk,khd->qhd', grad_scores, split_heads(key_rows))).reshape(row_count, HEADS * HEAD_DIM)
    grad_keys = rounded(jnp.einsum('hqk,qhd->khd', grad_scores, split_heads(queries))).reshape(row_count, HEADS * HEAD_DIM)
    group_width = HEADS * HEAD_DIM // N_TENSOR
    grad_norm = jnp.zeros(inputs.shape, jnp.float32)
    grad_source = jnp.zeros(inputs.shape, jnp.float32)
    for head_group in range(N_TENSOR):
        columns = slice(head_group * group_width, (head_group + 1) * group_width)
        query_part = jnp.dot(grad_query[:, columns], w_qkv[:, 0, columns].T, preferred_element_type=jnp.float32)
        source_part = jnp.dot(grad_keys[:, columns], w_qkv[:, 1, columns].T, preferred_element_type=jnp.float32)
        source_part = source_part + jnp.dot(grad_values[:, columns], w_qkv[:, 2, columns].T, preferred_element_type=jnp.float32)
        if crossing:
            grad_norm = grad_norm + rounded(query_part).astype(jnp.float32)
            grad_source = grad_source + source_part
        else:
            grad_norm = grad_norm + rounded(query_part + source_part).astype(jnp.float32)
    inverse = inverse_rms(inputs)
    scaled_grad = gain_row.astype(jnp.float32) * grad_norm
    result = upstream.astype(jnp.float32) + inverse * scaled_grad - inputs * inverse ** 3 * lax.optimization_barrier(jnp.mean(scaled_grad * inputs, axis=-1, keepdims=True))
    return (result.astype(jnp.bfloat16), grad_source)

def final_backward(saved, gain_row, gradients):
    inputs = saved.astype(jnp.float32)
    inverse = inverse_rms(inputs)
    scaled_grad = gain_row.astype(jnp.float32) * gradients
    return inverse * scaled_grad - inputs * inverse ** 3 * lax.optimization_barrier(jnp.mean(scaled_grad * inputs, axis=-1, keepdims=True))

def reference(fwd_in, bwd_in, cotangent, enc_saved, norm_gain, final_gain, w_qkv, w_out):

    def encode_layer(section_items):
        return forward(section_items[0], section_items[1], section_items[2], section_items[3], None)
    enc_outputs = lax.map(encode_layer, (fwd_in[:ENC_SECTIONS], norm_gain[:ENC_SECTIONS], w_qkv[:ENC_SECTIONS], w_out[:ENC_SECTIONS]))
    top_normed = normalize(enc_outputs[ENC_SECTIONS - 1].astype(jnp.float32), final_gain)

    def decode_layer(section_items):
        return forward(section_items[0], section_items[1], section_items[2], section_items[3], top_normed)
    dec_outputs = lax.map(decode_layer, (fwd_in[ENC_SECTIONS:], norm_gain[ENC_SECTIONS:], w_qkv[ENC_SECTIONS:], w_out[ENC_SECTIONS:]))
    outputs = jnp.concatenate([enc_outputs, dec_outputs], axis=0)
    arrived = jnp.roll(outputs, 1, axis=0)
    fwd_out = arrived.at[ENC_SECTIONS].set(jnp.zeros_like(arrived[0]))
    saved_normed = normalize(enc_saved.astype(jnp.float32), final_gain)

    def decode_back(section_items):
        return backward(section_items[0], section_items[1], section_items[2], section_items[3], section_items[4], saved_normed)
    dec_grads, dec_sources = lax.map(decode_back, (bwd_in[ENC_SECTIONS:], cotangent[ENC_SECTIONS:], norm_gain[ENC_SECTIONS:], w_qkv[ENC_SECTIONS:], w_out[ENC_SECTIONS:]))
    returned = final_backward(enc_saved, final_gain, lax.optimization_barrier(jnp.sum(dec_sources, axis=0))).astype(jnp.bfloat16)
    enc_upstream = cotangent[:ENC_SECTIONS].at[ENC_SECTIONS - 1].set(returned)

    def encode_back(section_items):
        return backward(section_items[0], section_items[1], section_items[2], section_items[3], section_items[4], None)[0]
    enc_grads = lax.map(encode_back, (bwd_in[:ENC_SECTIONS], enc_upstream, norm_gain[:ENC_SECTIONS], w_qkv[:ENC_SECTIONS], w_out[:ENC_SECTIONS]))
    grad_in = jnp.concatenate([enc_grads, dec_grads], axis=0)
    return (fwd_out, grad_in)
```

```python
import jax
import jax.numpy as jnp
from jax import lax
from jax.sharding import PartitionSpec as P

HEAD_DIM = 256
NY, NX, NZ, NC, NT = 4, 4, 2, 2, 4
SECTION_COUNT = NY * NX * NZ * NC
ENC_SECTIONS = SECTION_COUNT // 2
LAST = ENC_SECTIONS - 1

epsilon = 1e-06
f32 = jnp.float32
bf16 = jnp.bfloat16

PLACES = [
    (y, x, z, c, t)
    for y in range(NY)
    for x in range(NX)
    for z in range(NZ)
    for c in range(NC)
    for t in range(NT)
]


def place_index(place):
    y, x, z, c, t = place
    return (((y * NX + x) * NZ + z) * NC + c) * NT + t


def section_of(place):
    return place_index(place) // NT


def move(value, route):
    pairs = []
    for place in PLACES:
        target = route(*place)
        if target is not None:
            pairs.append((place_index(place), place_index(target)))
    return lax.ppermute(value, ("section", "tensor"), pairs)


def ring_slots(value, axis, size, only=None):
    def route(step):
        def go(*place):
            target = list(place)
            target[axis] = (place[axis] - step) % size
            if only is not None and not only(*target):
                return None
            return tuple(target)

        return go

    return [value] + [move(value, route(step)) for step in range(1, size)]


def line_gather(shard):
    right, left = shard, shard
    from_left, from_right = [], []
    for step in range(1, NT):
        right = move(right, lambda y, x, z, c, t: (y, x, z, c, t + 1) if step - 1 <= t < NT - 1 else None)
        left = move(left, lambda y, x, z, c, t: (y, x, z, c, t - 1) if 0 < t <= NT - step else None)
        from_left.append(right)
        from_right.append(left)
    t = lax.axis_index("tensor")
    slots = [shard]
    for k in range(1, NT):
        slots.append(jnp.where(t + k < NT, from_right[k - 1], from_left[NT - k - 1]))
    return jnp.concatenate(slots, axis=1)


def line_scatter(total):
    width = total.shape[1] // NT
    chunk = lambda k: total[:, k * width : (k + 1) * width].astype(f32)
    from_left = from_right = None
    for step in range(1, NT):
        right, left = chunk(NT - step), chunk(step)
        if step > 1:
            right, left = right + from_left.astype(f32), left + from_right.astype(f32)
        from_left = move(
            right.astype(bf16), lambda y, x, z, c, t: (y, x, z, c, t + 1) if t <= min(step - 1, NT - 2) else None
        )
        from_right = move(
            left.astype(bf16), lambda y, x, z, c, t: (y, x, z, c, t - 1) if t >= max(NT - step, 1) else None
        )
    return chunk(0) + from_left.astype(f32) + from_right.astype(f32)


def row_total(partial):
    rows = partial.shape[0]
    flat = partial.reshape(rows // 128, 128) if rows % 128 == 0 else partial.reshape(1, rows)
    return sum(ring_slots(flat, 4, NT)).reshape(rows, 1)


def inverse_rms(values):
    return lax.rsqrt(jnp.mean(values * values, axis=-1, keepdims=True) + epsilon)


def scale_rows(values, inverse, gain_row):
    return (values * inverse * gain_row).astype(bf16)


def mm(a, b):
    return jnp.dot(a, b, preferred_element_type=f32)


def mm_t(a, b):
    return lax.dot_general(a, b, (((1,), (1,)), ((), ())), preferred_element_type=f32)


def t_mm(a, b):
    return lax.dot_general(a, b, (((0,), (0,)), ((), ())), preferred_element_type=f32)


def heads_of(matrix):
    return [matrix[:, h * HEAD_DIM : (h + 1) * HEAD_DIM] for h in range(matrix.shape[1] // HEAD_DIM)]


def softmax_rows(queries, keys):
    weights = jnp.exp(mm_t(queries, keys) * HEAD_DIM ** (-0.5))
    return weights / jnp.sum(weights, axis=-1, keepdims=True)


def attend_out(q, k, v, w_proj):
    mixed = [
        mm(softmax_rows(qh, kh).astype(bf16), vh).astype(bf16)
        for qh, kh, vh in zip(heads_of(q), heads_of(k), heads_of(v))
    ]
    return mm(jnp.concatenate(mixed, axis=1), w_proj)


def attend_back(q, k, v, upstream, w_proj):
    grad_mix = mm_t(upstream, w_proj).astype(bf16)
    dq, dk, dv = [], [], []
    for qh, kh, vh, gh in zip(heads_of(q), heads_of(k), heads_of(v), heads_of(grad_mix)):
        weights = softmax_rows(qh, kh)
        dv.append(t_mm(weights.astype(bf16), gh).astype(bf16))
        grad_weights = mm_t(gh, vh)
        grad_scores = (
            weights
            * (grad_weights - jnp.sum(weights * grad_weights, axis=-1, keepdims=True))
            * HEAD_DIM ** (-0.5)
        ).astype(bf16)
        dq.append(mm(grad_scores, kh).astype(bf16))
        dk.append(t_mm(grad_scores, qh).astype(bf16))
    return [jnp.concatenate(parts, axis=1) for parts in (dq, dk, dv)]


def is_dec(y):
    return y >= NY // 2


def gather_rows(own):
    half = jnp.concatenate(ring_slots(own, 1, NX), axis=0)
    return jnp.concatenate(ring_slots(half, 3, NC), axis=0)


def body(fwd_in, bwd_in, cotangent, enc_saved, norm_gain, final_gain, w_qkv, w_out):
    section_index = lax.axis_index("section")
    t = lax.axis_index("tensor")
    core = section_index % NC
    x_at = section_index // (NC * NZ) % NX
    y_at = section_index // (NC * NZ * NX)
    dec = section_index >= ENC_SECTIONS
    last = section_index == LAST
    fwd_shard, bwd_shard, cot_shard = fwd_in[0], bwd_in[0], cotangent[0]
    rows, width = fwd_shard.shape
    full = width * NT
    part = rows // (NX * NC)

    a_full = line_gather(jnp.where(dec, bwd_shard, fwd_shard))
    gains = jnp.concatenate([norm_gain, final_gain[None]], axis=0)
    gains = jnp.concatenate(ring_slots(gains, 4, NT), axis=1).astype(f32)
    gain, final = gains[0:1], gains[1:2]
    own_rows = lax.dynamic_slice_in_dim(enc_saved, (x_at * NC + core) * part, part, 0)
    saved = jnp.concatenate(ring_slots(own_rows, 4, NT), axis=1).astype(f32)
    saved_inverse = inverse_rms(saved)
    saved_normed = gather_rows(scale_rows(saved, saved_inverse, final))
    b_full = line_gather(jnp.where(dec, cot_shard, bwd_shard))
    c_full = line_gather(jnp.where(dec, fwd_shard, cot_shard))

    order = [(t + k) % NT for k in range(NT)]
    w_in = w_qkv[0]
    turned = [lax.dynamic_slice_in_dim(w_in, o * width, width, 0) for o in order]
    w_q, w_k, w_v = (jnp.concatenate([w[:, i] for w in turned], axis=0) for i in range(3))
    w_o = jnp.concatenate([lax.dynamic_slice_in_dim(w_out[0], o * width, width, 1) for o in order], axis=1)

    a_values = a_full.astype(f32)
    a_inverse = inverse_rms(a_values)
    a_normed = scale_rows(a_values, a_inverse, gain)
    source = jnp.where(dec, saved_normed, a_normed)
    q1 = mm(a_normed, w_q).astype(bf16)
    k1 = mm(source, w_k).astype(bf16)
    v1 = mm(source, w_v).astype(bf16)

    def dec_back(_):
        dq, dk, dv = attend_back(q1, k1, v1, b_full, w_o)
        return mm_t(dq, w_q).astype(bf16), (mm_t(dk, w_k) + mm_t(dv, w_v)).astype(bf16)

    def enc_forward(_):
        return attend_out(q1, k1, v1, w_o).astype(bf16), jnp.zeros((rows, full), bf16)

    term1, dc = lax.cond(dec, dec_back, enc_forward, 0)

    def dec_only(route):
        return lambda y, x, z, c, tt: route(y, x, z, c, tt) if is_dec(y) else None

    half = rows // NC
    got = move(dc[half:], dec_only(lambda y, x, z, c, tt: (y, x, z, 1 - c, tt)))
    acc = dc[:half].astype(f32) + got.astype(f32)
    acc16 = acc.astype(bf16)
    total = acc[:part]
    for k in range(1, NX):
        total = total + move(
            acc16[k * part : (k + 1) * part], dec_only(lambda y, x, z, c, tt: (y, (x + k) % NX, z, c, tt))
        ).astype(f32)
    low = y_at % 2 == 0
    few = part // 2
    keep = jnp.where(low, total[:few], total[few:])
    give = jnp.where(low, total[few:], total[:few]).astype(bf16)
    keep = keep + move(give, dec_only(lambda y, x, z, c, tt: (y ^ 1, x, z, c, tt))).astype(f32)
    keep16 = keep.astype(bf16)
    mine = keep[:, :width]
    for k in range(1, NT):
        mine = mine + move(
            keep16[:, k * width : (k + 1) * width], dec_only(lambda y, x, z, c, tt: (y, x, z, c, (tt + k) % NT))
        ).astype(f32)
    mine = mine + move(mine, dec_only(lambda y, x, z, c, tt: (y, x, 1 - z, c, tt)))
    u = final * jnp.concatenate(ring_slots(mine, 4, NT, lambda y, x, z, c, tt: is_dec(y)), axis=1)
    e = jnp.where(low, saved[:few], saved[few:])
    r = jnp.where(low, saved_inverse[:few], saved_inverse[few:])
    returned = (r * u - e * r**3 * jnp.mean(u * e, axis=-1, keepdims=True)).astype(bf16)
    to_last = lambda frm: lambda y, x, z, c, tt: (1, x, z, c, tt) if (y == frm and z == 1) else None
    block = jnp.concatenate([move(returned, to_last(2)), move(returned, to_last(3))], axis=0)
    at_last = lambda y, x, z, c, tt: y == 1 and x == NX - 1 and z == 1
    slots = ring_slots(block, 1, NX, at_last)
    other = move(
        jnp.stack(slots), lambda y, x, z, c, tt: (y, x, z, 1, tt) if at_last(y, x, z, c, tt) and c == 0 else None
    )
    pieces = []
    for xi in range(NX):
        k = (xi - (NX - 1)) % NX
        pieces += [other[k], slots[k]]
    returned_full = jnp.concatenate(pieces, axis=0)

    summed1 = line_scatter(term1)
    enc_y = (fwd_shard.astype(f32) + summed1).astype(bf16)

    blocks = enc_y.reshape(NX, NC, part, width)
    is_last = lambda y, x, z, c, tt: section_of((y, x, z, c, tt)) == LAST
    passed = move(blocks[:, 0], lambda y, x, z, c, tt: (y, x, z, 0, tt) if is_last(y, x, z, c, tt) else None)
    blocks = jnp.where(core == 1, blocks[:, 1], passed)
    top = jnp.where(x_at == NX - 1, blocks[NX - 1], jnp.zeros_like(blocks[0]))
    for xi in range(NX - 1):
        top = top + move(
            blocks[xi], lambda y, x, z, c, tt: (y, xi, z, c, tt) if y == 1 and x == NX - 1 and z == 1 else None
        )
    arrivals = [
        move(top, lambda y, x, z, c, tt: (y_to, x, z_to, c, tt) if y == 1 and z == 1 else None)
        for y_to in (2, 3)
        for z_to in (0, 1)
    ]
    top = sum(arrivals)
    top = jnp.concatenate(ring_slots(top, 4, NT, lambda y, x, z, c, tt: is_dec(y)), axis=1).astype(f32)
    top_normed = scale_rows(top, inverse_rms(top), final)
    dec_slots = lambda v, axis, size: ring_slots(v, axis, size, lambda y, x, z, c, tt: is_dec(y))
    top_full = jnp.concatenate(dec_slots(top_normed, 1, NX), axis=0)
    top_full = jnp.concatenate(dec_slots(top_full, 3, NC), axis=0)

    b_values = jnp.where(dec, c_full, b_full).astype(f32)
    b_inverse = inverse_rms(b_values)
    b_normed = scale_rows(b_values, b_inverse, gain)
    q2 = mm(b_normed, w_q).astype(bf16)
    source2 = jnp.where(dec, top_full, b_normed)
    k2 = mm(source2, w_k).astype(bf16)
    v2 = mm(source2, w_v).astype(bf16)
    upstream = jnp.where(last, returned_full, c_full)

    def dec_forward(_):
        return attend_out(q2, k2, v2, w_o).astype(bf16)

    def enc_back(_):
        dq, dk, dv = attend_back(q2, k2, v2, upstream, w_o)
        return (mm_t(dq, w_q) + mm_t(dk, w_k) + mm_t(dv, w_v)).astype(bf16)

    term2 = lax.cond(dec, dec_forward, enc_back, 0)
    summed2 = line_scatter(term2)

    layer_out = jnp.where(dec, (fwd_shard.astype(f32) + summed2).astype(bf16), enc_y)

    def following(y, x, z, c, tt):
        s = section_of((y, x, z, c, tt))
        n = ((s + 1) % SECTION_COUNT) * NT + tt
        return None if s == LAST else PLACES[n]

    fwd_out = move(layer_out, following)[None]

    back_values = jnp.where(dec, a_values, b_values)
    back_term = jnp.where(dec, term1, term2).astype(f32)
    inverse = jnp.where(dec, a_inverse, b_inverse)
    summed = jnp.where(dec, summed1, summed2)
    row_sum = row_total(jnp.sum(gain * back_term * back_values, axis=-1))
    upstream_shard = jnp.where(last, returned_full[:, :width], cot_shard).astype(f32)
    grad_in = (
        upstream_shard
        + inverse * (gain[:, :width] * summed)
        - bwd_shard.astype(f32) * inverse**3 * (row_sum / full)
    ).astype(bf16)[None]
    return (fwd_out, grad_in)


def solution(mesh):
    in_specs = (
        P("section", None, "tensor"),
        P("section", None, "tensor"),
        P("section", None, "tensor"),
        P(None, "tensor"),
        P("section", "tensor"),
        P("tensor"),
        P("section", None, None, "tensor"),
        P("section", "tensor", None),
    )
    out_specs = (P("section", None, "tensor"), P("section", None, "tensor"))
    return jax.shard_map(body, mesh=mesh, in_specs=in_specs, out_specs=out_specs, check_vma=False)
```

```python
import jax
import jax.numpy as jnp
from jax import lax
from jax.sharding import PartitionSpec as P

HEAD_DIM = 256
NY, NX, NZ, NC, NT = 4, 4, 2, 2, 4
SECTION_COUNT = NY * NX * NZ * NC
ENC_SECTIONS = SECTION_COUNT // 2
LAST = ENC_SECTIONS - 1

epsilon = 1e-06
f32 = jnp.float32
bf16 = jnp.bfloat16

PLACES = [
    (y, x, z, c, t)
    for y in range(NY)
    for x in range(NX)
    for z in range(NZ)
    for c in range(NC)
    for t in range(NT)
]


def place_index(place):
    y, x, z, c, t = place
    return (((y * NX + x) * NZ + z) * NC + c) * NT + t


def section_of(place):
    return place_index(place) // NT


def move(value, route):
    pairs = []
    for place in PLACES:
        target = route(*place)
        if target is not None:
            pairs.append((place_index(place), place_index(target)))
    return lax.ppermute(value, ("section", "tensor"), pairs)


def ring_slots(value, axis, size, only=None):
    def route(step):
        def go(*place):
            target = list(place)
            target[axis] = (place[axis] - step) % size
            if only is not None and not only(*target):
                return None
            return tuple(target)

        return go

    return [value] + [move(value, route(step)) for step in range(1, size)]


def after(value, *others):
    return lax.optimization_barrier((value,) + others)[0]


def line_gathers(shards):
    t = lax.axis_index("tensor")
    ended = [()] * NT
    gathered = []
    for shard in shards:
        right, left = shard, shard
        from_left, from_right = [], []
        for step in range(1, NT):
            right, left = after(right, *ended[step]), after(left, *ended[step])
            right = move(right, lambda y, x, z, c, t: (y, x, z, c, t + 1) if step - 1 <= t < NT - 1 else None)
            left = move(left, lambda y, x, z, c, t: (y, x, z, c, t - 1) if 0 < t <= NT - step else None)
            ended[step] = (right, left)
            from_left.append(right)
            from_right.append(left)
        slots = [shard]
        for k in range(1, NT):
            slots.append(jnp.where(t + k < NT, from_right[k - 1], from_left[NT - k - 1]))
        gathered.append(jnp.concatenate(slots, axis=1))
    return gathered


def line_scatter(total):
    width = total.shape[1] // NT
    chunk = lambda k: total[:, k * width : (k + 1) * width].astype(f32)
    from_left = from_right = None
    for step in range(1, NT):
        right, left = chunk(NT - step), chunk(step)
        if step > 1:
            right, left = right + from_left.astype(f32), left + from_right.astype(f32)
        from_left = move(
            right.astype(bf16), lambda y, x, z, c, t: (y, x, z, c, t + 1) if t <= min(step - 1, NT - 2) else None
        )
        from_right = move(
            left.astype(bf16), lambda y, x, z, c, t: (y, x, z, c, t - 1) if t >= max(NT - step, 1) else None
        )
    return chunk(0) + from_left.astype(f32) + from_right.astype(f32)


def row_total(partial):
    rows = partial.shape[0]
    flat = partial.reshape(rows // 128, 128) if rows % 128 == 0 else partial.reshape(1, rows)
    return sum(ring_slots(flat, 4, NT)).reshape(rows, 1)


def inverse_rms(values):
    return lax.rsqrt(jnp.mean(values * values, axis=-1, keepdims=True) + epsilon)


def scale_rows(values, inverse, gain_row):
    return (values * inverse * gain_row).astype(bf16)


def mm(a, b):
    return jnp.dot(a, b, preferred_element_type=f32)


def mm_t(a, b):
    return lax.dot_general(a, b, (((1,), (1,)), ((), ())), preferred_element_type=f32)


def t_mm(a, b):
    return lax.dot_general(a, b, (((0,), (0,)), ((), ())), preferred_element_type=f32)


def heads_of(matrix):
    return [matrix[:, h * HEAD_DIM : (h + 1) * HEAD_DIM] for h in range(matrix.shape[1] // HEAD_DIM)]


def softmax_rows(queries, keys):
    weights = jnp.exp(mm_t(queries, keys) * HEAD_DIM ** (-0.5))
    return weights / jnp.sum(weights, axis=-1, keepdims=True)


def attend_out(q, k, v, w_proj):
    mixed = [
        mm(softmax_rows(qh, kh).astype(bf16), vh).astype(bf16)
        for qh, kh, vh in zip(heads_of(q), heads_of(k), heads_of(v))
    ]
    return mm(jnp.concatenate(mixed, axis=1), w_proj)


def attend_back(q, k, v, upstream, w_proj):
    grad_mix = mm_t(upstream, w_proj).astype(bf16)
    dq, dk, dv = [], [], []
    for qh, kh, vh, gh in zip(heads_of(q), heads_of(k), heads_of(v), heads_of(grad_mix)):
        weights = softmax_rows(qh, kh)
        dv.append(t_mm(weights.astype(bf16), gh).astype(bf16))
        grad_weights = mm_t(gh, vh)
        grad_scores = (
            weights
            * (grad_weights - jnp.sum(weights * grad_weights, axis=-1, keepdims=True))
            * HEAD_DIM ** (-0.5)
        ).astype(bf16)
        dq.append(mm(grad_scores, kh).astype(bf16))
        dk.append(t_mm(grad_scores, qh).astype(bf16))
    return [jnp.concatenate(parts, axis=1) for parts in (dq, dk, dv)]


def is_dec(y):
    return y >= NY // 2


def gather_rows(own):
    half = jnp.concatenate(ring_slots(own, 1, NX), axis=0)
    return jnp.concatenate([half, swap_core(half)], axis=0)


def swap_core(value):
    return move(value, lambda y, x, z, c, t: (y, x, z, 1 - c, t))


def turn(matrix, by):
    width = matrix.shape[1] // NT
    twice = jnp.concatenate([matrix, matrix], axis=1)
    return lax.dynamic_slice_in_dim(twice, by % NT * width, matrix.shape[1], 1)


def body(fwd_in, bwd_in, cotangent, enc_saved, norm_gain, final_gain, w_qkv, w_out):
    section_index = lax.axis_index("section")
    t = lax.axis_index("tensor")
    core = section_index % NC
    x_at = section_index // (NC * NZ) % NX
    y_at = section_index // (NC * NZ * NX)
    dec = section_index >= ENC_SECTIONS
    last = section_index == LAST
    fwd_shard, bwd_shard, cot_shard = fwd_in[0], bwd_in[0], cotangent[0]
    rows, width = fwd_shard.shape
    full = width * NT
    part = rows // (NX * NC)

    a_full, b_full, c_full = line_gathers(
        [
            jnp.where(dec, bwd_shard, fwd_shard),
            jnp.where(dec, cot_shard, bwd_shard),
            jnp.where(dec, fwd_shard, cot_shard),
        ]
    )
    own_rows = lax.dynamic_slice_in_dim(enc_saved, (x_at * NC + core) * part, part, 0)
    small = jnp.concatenate([own_rows, norm_gain, final_gain[None]], axis=0)
    small = jnp.concatenate(ring_slots(small, 4, NT), axis=1).astype(f32)
    saved, gain, final = small[:part], small[part : part + 1], small[part + 1 :]
    saved_inverse = inverse_rms(saved)
    saved_normed = gather_rows(scale_rows(saved, saved_inverse, final))

    order = [(t + k) % NT for k in range(NT)]
    w_in = w_qkv[0]
    turned = [lax.dynamic_slice_in_dim(w_in, o * width, width, 0) for o in order]
    w_q, w_k, w_v = (jnp.concatenate([w[:, i] for w in turned], axis=0) for i in range(3))
    w_o = jnp.concatenate([lax.dynamic_slice_in_dim(w_out[0], o * width, width, 1) for o in order], axis=1)

    a_values = a_full.astype(f32)
    a_inverse = inverse_rms(a_values)
    a_normed = scale_rows(a_values, a_inverse, gain)
    source = jnp.where(dec, saved_normed, a_normed)
    q1 = mm(a_normed, w_q).astype(bf16)
    k1 = mm(source, w_k).astype(bf16)
    v1 = mm(source, w_v).astype(bf16)

    def dec_back(_):
        dq, dk, dv = attend_back(q1, k1, v1, b_full, w_o)
        return mm_t(dq, w_q).astype(bf16), (mm_t(dk, w_k) + mm_t(dv, w_v)).astype(bf16)

    def enc_forward(_):
        return attend_out(q1, k1, v1, w_o).astype(bf16), jnp.zeros((rows, full), bf16)

    term1, dc = lax.cond(dec, dec_back, enc_forward, 0)
    summed1 = line_scatter(term1)
    enc_y = (fwd_shard.astype(f32) + summed1).astype(bf16)

    half = rows // NC
    acc = dc[:half].astype(f32) + swap_core(dc[half:]).astype(f32)
    acc16 = acc.astype(bf16)
    total = acc[:part]
    for k in range(1, NX):
        total = total + move(
            acc16[k * part : (k + 1) * part], lambda y, x, z, c, tt: (y, (x + k) % NX, z, c, tt)
        ).astype(f32)
    low = y_at % 2 == 0
    few = part // 2
    keep = jnp.where(low, total[:few], total[few:])
    give = jnp.where(low, total[few:], total[:few]).astype(bf16)
    keep = keep + move(give, lambda y, x, z, c, tt: (y ^ 1, x, z, c, tt)).astype(f32)
    keep = keep + move(
        keep.astype(bf16), lambda y, x, z, c, tt: (y, x, 1, c, tt) if z == 0 and is_dec(y) else None
    ).astype(f32)
    keep = turn(keep, -t)
    keep = keep + move(keep.astype(bf16), lambda y, x, z, c, tt: (y, x, z, c, tt ^ 1)).astype(f32)
    keep = keep + move(keep.astype(bf16), lambda y, x, z, c, tt: (y, x, z, c, (tt + 2) % NT)).astype(f32)
    u = final * turn(keep, t)
    e = jnp.where(low, saved[:few], saved[few:])
    r = jnp.where(low, saved_inverse[:few], saved_inverse[few:])
    returned = (r * u - e * r**3 * jnp.mean(u * e, axis=-1, keepdims=True)).astype(bf16)
    to_last = lambda frm: lambda y, x, z, c, tt: (1, x, z, c, tt) if (y == frm and z == 1) else None
    block = jnp.concatenate([move(returned, to_last(2)), move(returned, to_last(3))], axis=0)
    slots = jnp.concatenate(ring_slots(block, 1, NX), axis=0)
    other = swap_core(slots)
    pieces = []
    for xi in range(NX):
        k = (xi - (NX - 1)) % NX
        pieces += [other[k * part : (k + 1) * part], slots[k * part : (k + 1) * part]]
    returned_full = jnp.concatenate(pieces, axis=0)

    blocks = enc_y.reshape(NX, NC, part, width)
    blocks = jnp.where(core == 1, blocks[:, 1], swap_core(blocks[:, 0]))
    top = blocks[NX - 1]
    for k in range(1, NX):
        sent = move(blocks[k - 1], lambda y, x, z, c, tt: (y, (x + k) % NX, z, c, tt))
        top = jnp.where(x_at == k - 1, sent, top)
    arrivals = [
        move(top, lambda y, x, z, c, tt: (y_to, x, z_to, c, tt) if y == 1 and z == 1 else None)
        for y_to in (2, 3)
        for z_to in (0, 1)
    ]
    top = sum(arrivals)
    top = jnp.concatenate(ring_slots(top, 4, NT), axis=1).astype(f32)
    top_full = gather_rows(scale_rows(top, inverse_rms(top), final))

    b_values = jnp.where(dec, c_full, b_full).astype(f32)
    b_inverse = inverse_rms(b_values)
    b_normed = scale_rows(b_values, b_inverse, gain)
    q2 = mm(b_normed, w_q).astype(bf16)
    source2 = jnp.where(dec, top_full, b_normed)
    k2 = mm(source2, w_k).astype(bf16)
    v2 = mm(source2, w_v).astype(bf16)
    upstream = jnp.where(last, returned_full, c_full)

    def dec_forward(_):
        return attend_out(q2, k2, v2, w_o).astype(bf16)

    def enc_back(_):
        dq, dk, dv = attend_back(q2, k2, v2, upstream, w_o)
        return (mm_t(dq, w_q) + mm_t(dk, w_k) + mm_t(dv, w_v)).astype(bf16)

    term2 = lax.cond(dec, dec_forward, enc_back, 0)
    summed2 = line_scatter(term2)

    dec_y = (fwd_shard.astype(f32) + summed2).astype(bf16)

    def following(kind):
        def go(y, x, z, c, tt):
            s = section_of((y, x, z, c, tt))
            n = ((s + 1) % SECTION_COUNT) * NT + tt
            return None if s == LAST or is_dec(y) != kind else PLACES[n]

        return go

    fwd_out = (move(enc_y, following(False)) + move(dec_y, following(True)))[None]

    back_values = jnp.where(dec, a_values, b_values)
    back_term = jnp.where(dec, term1, term2).astype(f32)
    inverse = jnp.where(dec, a_inverse, b_inverse)
    summed = jnp.where(dec, summed1, summed2)
    row_sum = row_total(jnp.sum(gain * back_term * back_values, axis=-1))
    upstream_shard = jnp.where(last, returned_full[:, :width], cot_shard).astype(f32)
    grad_in = (
        upstream_shard
        + inverse * (gain[:, :width] * summed)
        - bwd_shard.astype(f32) * inverse**3 * (row_sum / full)
    ).astype(bf16)[None]
    return (fwd_out, grad_in)


def solution(mesh):
    in_specs = (
        P("section", None, "tensor"),
        P("section", None, "tensor"),
        P("section", None, "tensor"),
        P(None, "tensor"),
        P("section", "tensor"),
        P("tensor"),
        P("section", None, None, "tensor"),
        P("section", "tensor", None),
    )
    out_specs = (P("section", None, "tensor"), P("section", None, "tensor"))
    return jax.shard_map(body, mesh=mesh, in_specs=in_specs, out_specs=out_specs, check_vma=False)
```

```python
import jax
import jax.numpy as jnp
from jax import lax
from jax.sharding import PartitionSpec as P

HEAD_DIM = 256
NY, NX, NZ, NC, NT = 4, 4, 2, 2, 4
SECTION_COUNT = NY * NX * NZ * NC
ENC_SECTIONS = SECTION_COUNT // 2
LAST = ENC_SECTIONS - 1

epsilon = 1e-06
f32 = jnp.float32
bf16 = jnp.bfloat16

PLACES = [
    (y, x, z, c, t)
    for y in range(NY)
    for x in range(NX)
    for z in range(NZ)
    for c in range(NC)
    for t in range(NT)
]


def place_index(place):
    y, x, z, c, t = place
    return (((y * NX + x) * NZ + z) * NC + c) * NT + t


def section_of(place):
    return place_index(place) // NT


def move(value, route):
    pairs = []
    for place in PLACES:
        target = route(*place)
        if target is not None:
            pairs.append((place_index(place), place_index(target)))
    return lax.ppermute(value, ("section", "tensor"), pairs)


def ring_slots(value, axis, size, only=None):
    def route(step):
        def go(*place):
            target = list(place)
            target[axis] = (place[axis] - step) % size
            if only is not None and not only(*target):
                return None
            return tuple(target)

        return go

    return [value] + [move(value, route(step)) for step in range(1, size)]


def after(value, *others):
    return lax.optimization_barrier((value,) + others)[0]


def line_steps(shard):
    right, left = shard, shard
    steps = []
    for step in range(1, NT):
        waits = yield steps
        right, left = after(right, *waits), after(left, *waits)
        right = move(right, lambda y, x, z, c, t: (y, x, z, c, t + 1) if step - 1 <= t < NT - 1 else None)
        left = move(left, lambda y, x, z, c, t: (y, x, z, c, t - 1) if 0 < t <= NT - step else None)
        steps.append((right, left))
    yield steps


def start_gather(shard):
    steps = line_steps(shard)
    next(steps)
    return lambda *waits: steps.send(waits)[-1]


def joined(shard, steps):
    t = lax.axis_index("tensor")
    slots = [shard]
    for k in range(1, NT):
        slots.append(jnp.where(t + k < NT, steps[k - 1][1], steps[NT - k - 1][0]))
    return jnp.concatenate(slots, axis=1)


def line_scatter(total):
    width = total.shape[1] // NT
    chunk = lambda k: total[:, k * width : (k + 1) * width].astype(f32)
    from_left = from_right = None
    for step in range(1, NT):
        right, left = chunk(NT - step), chunk(step)
        if step > 1:
            right, left = right + from_left.astype(f32), left + from_right.astype(f32)
        from_left = move(right.astype(bf16), lambda y, x, z, c, t: (y, x, z, c, t + 1) if t < NT - 1 else None)
        from_right = move(left.astype(bf16), lambda y, x, z, c, t: (y, x, z, c, t - 1) if t > 0 else None)
    return chunk(0) + from_left.astype(f32) + from_right.astype(f32)


def row_total(partial):
    rows = partial.shape[0]
    flat = partial.reshape(rows // 128, 128) if rows % 128 == 0 else partial.reshape(1, rows)
    return sum(ring_slots(flat, 4, NT)).reshape(rows, 1)


def inverse_rms(values):
    return lax.rsqrt(jnp.mean(values * values, axis=-1, keepdims=True) + epsilon)


def scale_rows(values, inverse, gain_row):
    return (values * inverse * gain_row).astype(bf16)


def mm(a, b):
    return jnp.dot(a, b, preferred_element_type=f32)


def mm_t(a, b):
    return lax.dot_general(a, b, (((1,), (1,)), ((), ())), preferred_element_type=f32)


def t_mm(a, b):
    return lax.dot_general(a, b, (((0,), (0,)), ((), ())), preferred_element_type=f32)


def heads_of(matrix):
    return [matrix[:, h * HEAD_DIM : (h + 1) * HEAD_DIM] for h in range(matrix.shape[1] // HEAD_DIM)]


def softmax_rows(queries, keys):
    weights = jnp.exp(mm_t(queries, keys) * HEAD_DIM ** (-0.5))
    return weights / jnp.sum(weights, axis=-1, keepdims=True)


def attend_out(q, k, v, w_proj):
    mixed = [
        mm(softmax_rows(qh, kh).astype(bf16), vh).astype(bf16)
        for qh, kh, vh in zip(heads_of(q), heads_of(k), heads_of(v))
    ]
    return mm(jnp.concatenate(mixed, axis=1), w_proj)


def attend_back(q, k, v, upstream, w_proj):
    grad_mix = mm_t(upstream, w_proj).astype(bf16)
    dq, dk, dv = [], [], []
    for qh, kh, vh, gh in zip(heads_of(q), heads_of(k), heads_of(v), heads_of(grad_mix)):
        weights = softmax_rows(qh, kh)
        dv.append(t_mm(weights.astype(bf16), gh).astype(bf16))
        grad_weights = mm_t(gh, vh)
        grad_scores = (
            weights
            * (grad_weights - jnp.sum(weights * grad_weights, axis=-1, keepdims=True))
            * HEAD_DIM ** (-0.5)
        ).astype(bf16)
        dq.append(mm(grad_scores, kh).astype(bf16))
        dk.append(t_mm(grad_scores, qh).astype(bf16))
    return [jnp.concatenate(parts, axis=1) for parts in (dq, dk, dv)]


def is_dec(y):
    return y >= NY // 2


def gather_rows(own):
    half = jnp.concatenate(ring_slots(own, 1, NX), axis=0)
    return jnp.concatenate([half, swap_core(half)], axis=0)


def swap_core(value):
    return move(value, lambda y, x, z, c, t: (y, x, z, 1 - c, t))


def turn(matrix, by):
    width = matrix.shape[1] // NT
    twice = jnp.concatenate([matrix, matrix], axis=1)
    return lax.dynamic_slice_in_dim(twice, by % NT * width, matrix.shape[1], 1)


def body(fwd_in, bwd_in, cotangent, enc_saved, norm_gain, final_gain, w_qkv, w_out):
    section_index = lax.axis_index("section")
    t = lax.axis_index("tensor")
    core = section_index % NC
    x_at = section_index // (NC * NZ) % NX
    y_at = section_index // (NC * NZ * NX)
    dec = section_index >= ENC_SECTIONS
    last = section_index == LAST
    fwd_shard, bwd_shard, cot_shard = fwd_in[0], bwd_in[0], cotangent[0]
    rows, width = fwd_shard.shape
    full = width * NT
    part = rows // (NX * NC)

    a_shard = jnp.where(dec, bwd_shard, fwd_shard)
    b_shard = jnp.where(dec, cot_shard, bwd_shard)
    a_step, b_step = start_gather(a_shard), start_gather(b_shard)
    a1 = a_step()
    a2, b1 = a_step(), b_step(*a1)
    a3, b2 = a_step(*b1), b_step(*a2)
    b3 = b_step(*a3)
    a_full = after(joined(a_shard, [a1, a2, a3]), *b2)
    b_full = joined(b_shard, [b1, b2, b3])
    own_rows = lax.dynamic_slice_in_dim(enc_saved, (x_at * NC + core) * part, part, 0)
    small = jnp.concatenate([own_rows, norm_gain, final_gain[None]], axis=0)
    small = jnp.concatenate(ring_slots(small, 4, NT), axis=1).astype(f32)
    saved, gain, final = small[:part], small[part : part + 1], small[part + 1 :]
    saved_inverse = inverse_rms(saved)
    saved_normed = gather_rows(scale_rows(saved, saved_inverse, final))

    order = [(t + k) % NT for k in range(NT)]
    w_in = w_qkv[0]
    turned = [lax.dynamic_slice_in_dim(w_in, o * width, width, 0) for o in order]
    w_q, w_k, w_v = (jnp.concatenate([w[:, i] for w in turned], axis=0) for i in range(3))
    w_o = jnp.concatenate([lax.dynamic_slice_in_dim(w_out[0], o * width, width, 1) for o in order], axis=1)

    a_values = a_full.astype(f32)
    a_inverse = inverse_rms(a_values)
    a_normed = scale_rows(a_values, a_inverse, gain)
    source = jnp.where(dec, saved_normed, a_normed)
    q1 = mm(a_normed, w_q).astype(bf16)
    k1 = mm(source, w_k).astype(bf16)
    v1 = mm(source, w_v).astype(bf16)

    out1 = attend_out(q1, k1, v1, w_o).astype(bf16)

    def dec_back(_):
        dq, dk, dv = attend_back(q1, k1, v1, b_full, w_o)
        return mm_t(dq, w_q).astype(bf16), (mm_t(dk, w_k) + mm_t(dv, w_v)).astype(bf16)

    def no_back(_):
        return jnp.zeros((rows, full), bf16), jnp.zeros((rows, full), bf16)

    dec_dn, dc = lax.cond(dec, dec_back, no_back, 0)
    term1 = jnp.where(dec, dec_dn, out1)
    summed1 = line_scatter(term1)
    enc_y = (fwd_shard.astype(f32) + summed1).astype(bf16)
    c_shard = jnp.where(dec, fwd_shard, cot_shard)
    c_step = start_gather(c_shard)
    c_steps = [c_step(summed1), c_step(), c_step()]
    c_full = joined(c_shard, c_steps)

    def following(kind):
        def go(y, x, z, c, tt):
            s = section_of((y, x, z, c, tt))
            n = ((s + 1) % SECTION_COUNT) * NT + tt
            return None if s == LAST or is_dec(y) != kind else PLACES[n]

        return go

    enc_sent = move(enc_y, following(False))

    half = rows // NC
    acc = dc[:half].astype(f32) + swap_core(dc[half:]).astype(f32)
    acc16 = acc.astype(bf16)
    total = acc[:part]
    for k in range(1, NX):
        total = total + move(
            acc16[k * part : (k + 1) * part], lambda y, x, z, c, tt: (y, (x + k) % NX, z, c, tt)
        ).astype(f32)
    low = y_at % 2 == 0
    few = part // 2
    keep = jnp.where(low, total[:few], total[few:])
    give = jnp.where(low, total[few:], total[:few]).astype(bf16)
    keep = keep + move(give, lambda y, x, z, c, tt: (y ^ 1, x, z, c, tt)).astype(f32)
    keep = keep + move(
        keep.astype(bf16), lambda y, x, z, c, tt: (y, x, 1, c, tt) if z == 0 and is_dec(y) else None
    ).astype(f32)
    keep = turn(keep, -t)
    keep = keep + move(keep.astype(bf16), lambda y, x, z, c, tt: (y, x, z, c, tt ^ 1)).astype(f32)
    keep = keep + move(keep.astype(bf16), lambda y, x, z, c, tt: (y, x, z, c, (tt + 2) % NT)).astype(f32)
    u = final * turn(keep, t)
    e = jnp.where(low, saved[:few], saved[few:])
    r = jnp.where(low, saved_inverse[:few], saved_inverse[few:])
    returned = (r * u - e * r**3 * jnp.mean(u * e, axis=-1, keepdims=True)).astype(bf16)
    to_last = lambda frm: lambda y, x, z, c, tt: (1, x, z, c, tt) if (y == frm and z == 1) else None
    block = jnp.concatenate([move(returned, to_last(2)), move(returned, to_last(3))], axis=0)
    slots = jnp.concatenate(ring_slots(block, 1, NX), axis=0)
    other = swap_core(slots)
    pieces = []
    for xi in range(NX):
        k = (xi - (NX - 1)) % NX
        pieces += [other[k * part : (k + 1) * part], slots[k * part : (k + 1) * part]]
    returned_full = jnp.concatenate(pieces, axis=0)

    blocks = enc_y.reshape(NX, NC, part, width)
    blocks = jnp.where(core == 1, blocks[:, 1], swap_core(blocks[:, 0]))
    top = blocks[NX - 1]
    for k in range(1, NX):
        sent = move(blocks[k - 1], lambda y, x, z, c, tt: (y, (x + k) % NX, z, c, tt))
        top = jnp.where(x_at == k - 1, sent, top)
    arrivals = [
        move(top, lambda y, x, z, c, tt: (y_to, x, z_to, c, tt) if y == 1 and z == 1 else None)
        for y_to in (2, 3)
        for z_to in (0, 1)
    ]
    top = sum(arrivals)
    top = jnp.concatenate(ring_slots(top, 4, NT), axis=1).astype(f32)
    top_full = gather_rows(scale_rows(top, inverse_rms(top), final))

    b_values = jnp.where(dec, c_full, b_full).astype(f32)
    b_inverse = inverse_rms(b_values)
    b_normed = scale_rows(b_values, b_inverse, gain)
    q2 = mm(b_normed, w_q).astype(bf16)
    source2 = after(jnp.where(dec, top_full, b_normed), enc_sent)
    k2 = mm(source2, w_k).astype(bf16)
    v2 = mm(source2, w_v).astype(bf16)
    upstream = jnp.where(last, returned_full, c_full)

    def dec_forward(_):
        return attend_out(q2, k2, v2, w_o).astype(bf16)

    def enc_back(_):
        dq, dk, dv = attend_back(q2, k2, v2, upstream, w_o)
        return (mm_t(dq, w_q) + mm_t(dk, w_k) + mm_t(dv, w_v)).astype(bf16)

    term2 = lax.cond(dec, dec_forward, enc_back, 0)
    summed2 = line_scatter(term2)

    dec_y = (fwd_shard.astype(f32) + summed2).astype(bf16)

    fwd_out = (enc_sent + move(dec_y, following(True)))[None]

    back_values = jnp.where(dec, a_values, b_values)
    back_term = jnp.where(dec, term1, term2).astype(f32)
    inverse = jnp.where(dec, a_inverse, b_inverse)
    summed = jnp.where(dec, summed1, summed2)
    row_sum = row_total(jnp.sum(gain * back_term * back_values, axis=-1))
    upstream_shard = jnp.where(last, returned_full[:, :width], cot_shard).astype(f32)
    grad_in = (
        upstream_shard
        + inverse * (gain[:, :width] * summed)
        - bwd_shard.astype(f32) * inverse**3 * (row_sum / full)
    ).astype(bf16)[None]
    return (fwd_out, grad_in)


def solution(mesh):
    in_specs = (
        P("section", None, "tensor"),
        P("section", None, "tensor"),
        P("section", None, "tensor"),
        P(None, "tensor"),
        P("section", "tensor"),
        P("tensor"),
        P("section", None, None, "tensor"),
        P("section", "tensor", None),
    )
    out_specs = (P("section", None, "tensor"), P("section", None, "tensor"))
    return jax.shard_map(body, mesh=mesh, in_specs=in_specs, out_specs=out_specs, check_vma=False)
```

```python
import jax
import jax.numpy as jnp
from jax import lax
from jax.sharding import PartitionSpec as P

HEAD_DIM = 256
NY, NX, NZ, NC, NT = 4, 4, 2, 2, 4
SECTION_COUNT = NY * NX * NZ * NC
ENC_SECTIONS = SECTION_COUNT // 2
LAST = ENC_SECTIONS - 1

epsilon = 1e-06
f32 = jnp.float32
bf16 = jnp.bfloat16

PLACES = [
    (y, x, z, c, t)
    for y in range(NY)
    for x in range(NX)
    for z in range(NZ)
    for c in range(NC)
    for t in range(NT)
]


def place_index(place):
    y, x, z, c, t = place
    return (((y * NX + x) * NZ + z) * NC + c) * NT + t


def section_of(place):
    return place_index(place) // NT


def move(value, route):
    pairs = []
    for place in PLACES:
        target = route(*place)
        if target is not None:
            pairs.append((place_index(place), place_index(target)))
    return lax.ppermute(value, ("section", "tensor"), pairs)


def swap_x(value, k):
    return move(value, lambda y, x, z, c, t: (y, x ^ k, z, c, t))


def swap_core(value):
    return move(value, lambda y, x, z, c, t: (y, x, z, 1 - c, t))


def swap_t(value, k):
    return move(value, lambda y, x, z, c, t: (y, x, z, c, t ^ k))


def after(value, *others):
    return lax.optimization_barrier((value,) + others)[0]


def line_scatter(total, row_part):
    rows, width = total.shape[0], total.shape[1] // NT
    high = row_part.astype(bf16)
    low = (row_part - high.astype(f32)).astype(bf16)
    extra = jnp.concatenate([high, low]).reshape(1, 2 * rows)
    extra = jnp.pad(extra, ((0, 0), (0, 2 * width - 2 * rows))) if 2 * rows < 2 * width else extra
    got = swap_t(jnp.concatenate([total[:, 2 * width :], extra], axis=0), 1).astype(f32)
    pair = total[:, : 2 * width].astype(f32) + got[:rows]
    sums = row_part + got[rows, :rows] + got[rows, rows : 2 * rows]
    high = sums.astype(bf16)
    low = (sums - high.astype(f32)).astype(bf16)
    extra = jnp.concatenate([high, low]).reshape(2 * rows // width, width)
    got = swap_t(jnp.concatenate([pair[:, width:].astype(bf16), extra], axis=0), 2).astype(f32)
    tail = got[rows:].reshape(2 * rows)
    return pair[:, :width] + got[:rows], (sums + tail[:rows] + tail[rows:]).reshape(rows, 1)


def inverse_rms(values):
    return lax.rsqrt(jnp.mean(values * values, axis=-1, keepdims=True) + epsilon)


def scale_rows(values, inverse, gain_row):
    return (values * inverse * gain_row).astype(bf16)


def mm(a, b):
    return jnp.dot(a, b, preferred_element_type=f32)


def mm_t(a, b):
    return lax.dot_general(a, b, (((1,), (1,)), ((), ())), preferred_element_type=f32)


def t_mm(a, b):
    return lax.dot_general(a, b, (((0,), (0,)), ((), ())), preferred_element_type=f32)


def heads_of(matrix):
    return [matrix[:, h * HEAD_DIM : (h + 1) * HEAD_DIM] for h in range(matrix.shape[1] // HEAD_DIM)]


def softmax_rows(queries, keys):
    weights = jnp.exp(mm_t(queries, keys) * HEAD_DIM ** (-0.5))
    return weights / jnp.sum(weights, axis=-1, keepdims=True)


def attend_out(q, k, v, w_proj):
    mixed = [
        mm(softmax_rows(qh, kh).astype(bf16), vh).astype(bf16)
        for qh, kh, vh in zip(heads_of(q), heads_of(k), heads_of(v))
    ]
    return mm(jnp.concatenate(mixed, axis=1), w_proj)


def attend_back(q, k, v, upstream, w_proj):
    grad_mix = mm_t(upstream, w_proj).astype(bf16)
    dq, dk, dv = [], [], []
    for qh, kh, vh, gh in zip(heads_of(q), heads_of(k), heads_of(v), heads_of(grad_mix)):
        weights = softmax_rows(qh, kh)
        dv.append(t_mm(weights.astype(bf16), gh).astype(bf16))
        grad_weights = mm_t(gh, vh)
        grad_scores = (
            weights
            * (grad_weights - jnp.sum(weights * grad_weights, axis=-1, keepdims=True))
            * HEAD_DIM ** (-0.5)
        ).astype(bf16)
        dq.append(mm(grad_scores, kh).astype(bf16))
        dk.append(t_mm(grad_scores, qh).astype(bf16))
    return [jnp.concatenate(parts, axis=1) for parts in (dq, dk, dv)]


def is_dec(y):
    return y >= NY // 2


def gather_rows(own):
    half = jnp.concatenate([own] + [swap_x(own, k) for k in range(1, NX)], axis=0)
    return jnp.concatenate([half, swap_core(half)], axis=0)


def body(fwd_in, bwd_in, cotangent, enc_saved, norm_gain, final_gain, w_qkv, w_out):
    section_index = lax.axis_index("section")
    t = lax.axis_index("tensor")
    core = section_index % NC
    x_at = section_index // (NC * NZ) % NX
    y_at = section_index // (NC * NZ * NX)
    dec = section_index >= ENC_SECTIONS
    last = section_index == LAST
    fwd_shard, bwd_shard, cot_shard = fwd_in[0], bwd_in[0], cotangent[0]
    rows, width = fwd_shard.shape
    full = width * NT
    part = rows // (NX * NC)

    own_rows = lax.dynamic_slice_in_dim(enc_saved, (x_at * NC + core) * part, part, 0)
    a_shard = jnp.concatenate(
        [jnp.where(dec, bwd_shard, fwd_shard), own_rows, norm_gain, final_gain[None]], axis=0
    )
    b_shard = jnp.where(dec, cot_shard, bwd_shard)
    c_shard = jnp.where(dec, fwd_shard, cot_shard)
    a_far = swap_t(a_shard, 2)
    a_pair = jnp.concatenate([a_shard, a_far], axis=1)
    b_far = swap_t(after(b_shard, a_far), 2)
    a_near = swap_t(a_pair, 1)
    b_pair = jnp.concatenate([b_shard, b_far], axis=1)
    b_near = swap_t(after(b_pair, a_near), 1)
    a_all = jnp.concatenate([a_pair, a_near], axis=1)
    b_full = jnp.concatenate([b_pair, b_near], axis=1)
    a_full = a_all[:rows]
    small = a_all[rows:].astype(f32)
    saved, gain, final = small[:part], small[part : part + 1], small[part + 1 :]
    saved_inverse = inverse_rms(saved)
    saved_normed = gather_rows(scale_rows(saved, saved_inverse, final))

    order = [t, t ^ 2, t ^ 1, t ^ 3]
    w_in = w_qkv[0]
    turned = [lax.dynamic_slice_in_dim(w_in, o * width, width, 0) for o in order]
    w_q, w_k, w_v = (jnp.concatenate([w[:, i] for w in turned], axis=0) for i in range(3))
    w_o = jnp.concatenate([lax.dynamic_slice_in_dim(w_out[0], o * width, width, 1) for o in order], axis=1)

    a_values = a_full.astype(f32)
    a_inverse = inverse_rms(a_values)
    a_normed = scale_rows(a_values, a_inverse, gain)
    source = jnp.where(dec, saved_normed, a_normed)
    q1 = mm(a_normed, w_q).astype(bf16)
    k1 = mm(source, w_k).astype(bf16)
    v1 = mm(source, w_v).astype(bf16)

    out1 = attend_out(q1, k1, v1, w_o).astype(bf16)

    def dec_back(_):
        dq, dk, dv = attend_back(q1, k1, v1, b_full, w_o)
        return mm_t(dq, w_q).astype(bf16), (mm_t(dk, w_k) + mm_t(dv, w_v)).astype(bf16)

    def no_back(_):
        return jnp.zeros((rows, full), bf16), jnp.zeros((rows, full), bf16)

    dec_dn, dc = lax.cond(dec, dec_back, no_back, 0)
    term1 = jnp.where(dec, dec_dn, out1)
    summed1, row_sum1 = line_scatter(term1, jnp.sum(gain * term1.astype(f32) * a_values, axis=-1))
    enc_y = (fwd_shard.astype(f32) + summed1).astype(bf16)
    c_far = swap_t(after(c_shard, summed1), 2)

    def following(kind):
        def go(y, x, z, c, tt):
            s = section_of((y, x, z, c, tt))
            n = ((s + 1) % SECTION_COUNT) * NT + tt
            return None if s == LAST or is_dec(y) != kind else PLACES[n]

        return go

    half = rows // NC
    acc = dc[:half].astype(f32) + swap_core(dc[half:]).astype(f32)
    acc16 = acc.astype(bf16)
    total = acc[:part]
    for k in range(1, NX):
        total = total + swap_x(acc16[k * part : (k + 1) * part], k).astype(f32)
    low = y_at % 2 == 0
    few = part // 2
    keep = jnp.where(low, total[:few], total[few:])
    give = jnp.where(low, total[few:], total[:few]).astype(bf16)
    keep = keep + move(give, lambda y, x, z, c, tt: (y ^ 1, x, z, c, tt)).astype(f32)
    keep = keep + move(
        keep.astype(bf16), lambda y, x, z, c, tt: (y, x, 1, c, tt) if z == 0 and is_dec(y) else None
    ).astype(f32)
    got = swap_t(keep.astype(bf16), 1).astype(f32)
    keep = keep + jnp.concatenate([got[:, 2 * width :], got[:, : 2 * width]], axis=1)
    got = swap_t(keep.astype(bf16), 2).astype(f32)
    keep = keep + jnp.concatenate([got[:, o * width : (o + 1) * width] for o in (1, 0, 3, 2)], axis=1)
    u = final * keep
    e = jnp.where(low, saved[:few], saved[few:])
    r = jnp.where(low, saved_inverse[:few], saved_inverse[few:])
    returned = (r * u - e * r**3 * jnp.mean(u * e, axis=-1, keepdims=True)).astype(bf16)
    to_last = lambda frm: lambda y, x, z, c, tt: (1, x, z, c, tt) if (y == frm and z == 1) else None
    block = jnp.concatenate([move(returned, to_last(2)), move(returned, to_last(3))], axis=0)
    slots = jnp.concatenate([block] + [swap_x(block, k) for k in range(1, NX)], axis=0)
    other = swap_core(slots)
    pieces = []
    for xi in range(NX):
        k = xi ^ (NX - 1)
        pieces += [other[k * part : (k + 1) * part], slots[k * part : (k + 1) * part]]
    returned_full = jnp.concatenate(pieces, axis=0)

    blocks = enc_y.reshape(NX, NC, part, width)
    blocks = jnp.where(core == 1, blocks[:, 1], swap_core(blocks[:, 0]))
    top = blocks[NX - 1]
    for k in range(1, NX):
        top = jnp.where(x_at ^ (NX - 1) == k, swap_x(blocks[(NX - 1) ^ k], k), top)
    arrivals = [
        move(top, lambda y, x, z, c, tt: (y_to, x, z_to, c, tt) if y == 1 and z == 1 else None)
        for y_to in (2, 3)
        for z_to in (0, 1)
    ]
    top = sum(arrivals)
    top = jnp.concatenate([top, swap_t(top, 2)], axis=1)
    top = jnp.concatenate([top, swap_t(top, 1)], axis=1).astype(f32)
    top_full = gather_rows(scale_rows(top, inverse_rms(top), final))
    c_pair = jnp.concatenate([c_shard, c_far], axis=1)
    c_full = jnp.concatenate([c_pair, swap_t(after(c_pair, top), 1)], axis=1)
    enc_sent = move(after(enc_y, top), following(False))

    b_values = jnp.where(dec, c_full, b_full).astype(f32)
    b_inverse = inverse_rms(b_values)
    b_normed = after(scale_rows(b_values, b_inverse, gain), enc_sent)
    q2 = mm(b_normed, w_q).astype(bf16)
    source2 = jnp.where(dec, top_full, b_normed)
    k2 = mm(source2, w_k).astype(bf16)
    v2 = mm(source2, w_v).astype(bf16)
    upstream = jnp.where(last, returned_full, c_full)

    def dec_forward(_):
        return attend_out(q2, k2, v2, w_o).astype(bf16)

    def enc_back(_):
        dq, dk, dv = attend_back(q2, k2, v2, upstream, w_o)
        return (mm_t(dq, w_q) + mm_t(dk, w_k) + mm_t(dv, w_v)).astype(bf16)

    term2 = lax.cond(dec, dec_forward, enc_back, 0)
    summed2, row_sum2 = line_scatter(term2, jnp.sum(gain * term2.astype(f32) * b_values, axis=-1))

    dec_y = (fwd_shard.astype(f32) + summed2).astype(bf16)

    fwd_out = (enc_sent + move(dec_y, following(True)))[None]

    inverse = jnp.where(dec, a_inverse, b_inverse)
    summed = jnp.where(dec, summed1, summed2)
    row_sum = jnp.where(dec, row_sum1, row_sum2)
    upstream_shard = jnp.where(last, returned_full[:, :width], cot_shard).astype(f32)
    grad_in = (
        upstream_shard
        + inverse * (gain[:, :width] * summed)
        - bwd_shard.astype(f32) * inverse**3 * (row_sum / full)
    ).astype(bf16)[None]
    return (fwd_out, grad_in)


def solution(mesh):
    in_specs = (
        P("section", None, "tensor"),
        P("section", None, "tensor"),
        P("section", None, "tensor"),
        P(None, "tensor"),
        P("section", "tensor"),
        P("tensor"),
        P("section", None, None, "tensor"),
        P("section", "tensor", None),
    )
    out_specs = (P("section", None, "tensor"), P("section", None, "tensor"))
    return jax.shard_map(body, mesh=mesh, in_specs=in_specs, out_specs=out_specs, check_vma=False)
```

```python
import jax
import jax.numpy as jnp
from jax import lax
from jax.sharding import PartitionSpec as P

HEAD_DIM = 256
NY, NX, NZ, NC, NT = 4, 4, 2, 2, 4
SECTION_COUNT = NY * NX * NZ * NC
ENC_SECTIONS = SECTION_COUNT // 2
LAST = ENC_SECTIONS - 1

epsilon = 1e-06
f32 = jnp.float32
bf16 = jnp.bfloat16

PLACES = [
    (y, x, z, c, t)
    for y in range(NY)
    for x in range(NX)
    for z in range(NZ)
    for c in range(NC)
    for t in range(NT)
]


def place_index(place):
    y, x, z, c, t = place
    return (((y * NX + x) * NZ + z) * NC + c) * NT + t


def section_of(place):
    return place_index(place) // NT


def move(value, route):
    pairs = []
    for place in PLACES:
        target = route(*place)
        if target is not None:
            pairs.append((place_index(place), place_index(target)))
    return lax.ppermute(value, ("section", "tensor"), pairs)


def is_dec(y):
    return y >= NY // 2


def everyone(y, z):
    return True


def encoders(y, z):
    return y < NY // 2


def decoders(y, z):
    return y >= NY // 2


def top_row(y, z):
    return y == 1 and z == 1


def swap_x(value, k, who):
    return move(value, lambda y, x, z, c, t: (y, x ^ k, z, c, t) if who(y, z) else None)


def swap_core(value, who):
    return move(value, lambda y, x, z, c, t: (y, x, z, 1 - c, t) if who(y, z) else None)


def swap_t(value, k, who):
    return move(value, lambda y, x, z, c, t: (y, x, z, c, t ^ k) if who(y, z) else None)


def after(value, *others):
    return lax.optimization_barrier((value,) + others)[0]


def tie(value, other):
    return lax.optimization_barrier((value, other))


def line_scatter(total, row_part, who):
    rows, width = total.shape[0], total.shape[1] // NT
    give = total[:, 2 * width :]
    if row_part is not None:
        high = row_part.astype(bf16)
        low = (row_part - high.astype(f32)).astype(bf16)
        extra = jnp.concatenate([high, low]).reshape(1, 2 * rows)
        extra = jnp.pad(extra, ((0, 0), (0, 2 * width - 2 * rows))) if 2 * rows < 2 * width else extra
        give = jnp.concatenate([give, extra], axis=0)
    got = swap_t(give, 1, who).astype(f32)
    pair = total[:, : 2 * width].astype(f32) + got[:rows]
    give = pair[:, width:].astype(bf16)
    if row_part is not None:
        sums = row_part + got[rows, :rows] + got[rows, rows : 2 * rows]
        high = sums.astype(bf16)
        low = (sums - high.astype(f32)).astype(bf16)
        extra = jnp.concatenate([high, low]).reshape(2 * rows // width, width)
        give = jnp.concatenate([give, extra], axis=0)
    got = swap_t(give, 2, who).astype(f32)
    summed = pair[:, :width] + got[:rows]
    if row_part is None:
        return summed, None
    tail = got[rows:].reshape(2 * rows)
    return summed, (sums + tail[:rows] + tail[rows:]).reshape(rows, 1)


def inverse_rms(values):
    return lax.rsqrt(jnp.mean(values * values, axis=-1, keepdims=True) + epsilon)


def scale_rows(values, inverse, gain_row):
    return (values * inverse * gain_row).astype(bf16)


def mm(a, b):
    return jnp.dot(a, b, preferred_element_type=f32)


def mm_t(a, b):
    return lax.dot_general(a, b, (((1,), (1,)), ((), ())), preferred_element_type=f32)


def t_mm(a, b):
    return lax.dot_general(a, b, (((0,), (0,)), ((), ())), preferred_element_type=f32)


def heads_of(matrix):
    return [matrix[:, h * HEAD_DIM : (h + 1) * HEAD_DIM] for h in range(matrix.shape[1] // HEAD_DIM)]


def softmax_rows(queries, keys):
    weights = jnp.exp(mm_t(queries, keys) * HEAD_DIM ** (-0.5))
    return weights / jnp.sum(weights, axis=-1, keepdims=True)


def attend_out(q, k, v, w_proj):
    mixed = [
        mm(softmax_rows(qh, kh).astype(bf16), vh).astype(bf16)
        for qh, kh, vh in zip(heads_of(q), heads_of(k), heads_of(v))
    ]
    return mm(jnp.concatenate(mixed, axis=1), w_proj)


def attend_back(q, k, v, upstream, w_proj):
    grad_mix = mm_t(upstream, w_proj).astype(bf16)
    dq, dk, dv = [], [], []
    for qh, kh, vh, gh in zip(heads_of(q), heads_of(k), heads_of(v), heads_of(grad_mix)):
        weights = softmax_rows(qh, kh)
        dv.append(t_mm(weights.astype(bf16), gh).astype(bf16))
        grad_weights = mm_t(gh, vh)
        grad_scores = (
            weights
            * (grad_weights - jnp.sum(weights * grad_weights, axis=-1, keepdims=True))
            * HEAD_DIM ** (-0.5)
        ).astype(bf16)
        dq.append(mm(grad_scores, kh).astype(bf16))
        dk.append(t_mm(grad_scores, qh).astype(bf16))
    return [jnp.concatenate(parts, axis=1) for parts in (dq, dk, dv)]


def gather_rows(own, who):
    half = jnp.concatenate([own] + [swap_x(own, k, who) for k in range(1, NX)], axis=0)
    return jnp.concatenate([half, swap_core(half, who)], axis=0)


def following(kind):
    def go(y, x, z, c, t):
        s = section_of((y, x, z, c, t))
        n = ((s + 1) % SECTION_COUNT) * NT + t
        return None if s == LAST or is_dec(y) != kind else PLACES[n]

    return go


def body(fwd_in, bwd_in, cotangent, enc_saved, norm_gain, final_gain, w_qkv, w_out):
    section_index = lax.axis_index("section")
    t = lax.axis_index("tensor")
    core = section_index % NC
    x_at = section_index // (NC * NZ) % NX
    dec = section_index >= ENC_SECTIONS
    last = section_index == LAST
    fwd_shard, bwd_shard, cot_shard = fwd_in[0], bwd_in[0], cotangent[0]
    rows, width = fwd_shard.shape
    full = width * NT
    part = rows // (NX * NC)
    half = rows // NC

    own_rows = lax.dynamic_slice_in_dim(enc_saved, (x_at * NC + core) * part, part, 0)
    a_shard = jnp.concatenate(
        [jnp.where(dec, bwd_shard, fwd_shard), own_rows, norm_gain, final_gain[None]], axis=0
    )
    b_shard = jnp.where(dec, cot_shard, bwd_shard)
    a_far = swap_t(a_shard, 2, everyone)
    a_pair = jnp.concatenate([a_shard, a_far], axis=1)
    b_far = swap_t(after(b_shard, a_far), 2, everyone)
    a_near = swap_t(a_pair, 1, everyone)
    b_pair = jnp.concatenate([b_shard, b_far], axis=1)
    a_all = jnp.concatenate([a_pair, a_near], axis=1)
    small = a_all[rows:].astype(f32)
    saved, gain, final = small[:part], small[part : part + 1], small[part + 1 :]

    order = [t, t ^ 2, t ^ 1, t ^ 3]
    w_in = w_qkv[0]
    turned = [lax.dynamic_slice_in_dim(w_in, o * width, width, 0) for o in order]
    w_q, w_k, w_v = (jnp.concatenate([w[:, i] for w in turned], axis=0) for i in range(3))
    w_o = jnp.concatenate([lax.dynamic_slice_in_dim(w_out[0], o * width, width, 1) for o in order], axis=1)

    a_values = a_all[:rows].astype(f32)
    a_inverse = inverse_rms(a_values)
    a_normed = scale_rows(a_values, a_inverse, gain)
    def project(normed, source):
        return mm(normed, w_q).astype(bf16), mm(source, w_k).astype(bf16), mm(source, w_v).astype(bf16)

    def enc_phase1(_):
        b_near = swap_t(b_pair, 1, encoders)
        out = attend_out(*project(a_normed, a_normed), w_o).astype(bf16)
        out, b_near = tie(out, b_near)
        summed, _ = line_scatter(out, None, encoders)
        enc_y = (fwd_shard.astype(f32) + summed).astype(bf16)
        blocks = enc_y.reshape(NX, NC, part, width)
        passed, c_shard = tie(swap_core(blocks[:, 0], top_row), cot_shard)
        blocks = jnp.where(core == 1, blocks[:, 1], passed)
        c_far = swap_t(c_shard, 2, encoders)
        top = blocks[NX - 1]
        for k in range(1, NX):
            top = jnp.where(x_at ^ (NX - 1) == k, swap_x(blocks[(NX - 1) ^ k], k, top_row), top)
        return enc_y, top, b_near, c_far, out, out[:part]

    def dec_phase1(_):
        b_near = swap_t(b_pair, 1, decoders)
        c_far = swap_t(fwd_shard, 2, decoders)
        q = mm(a_normed, w_q).astype(bf16)
        saved_rows, q = tie(scale_rows(saved, inverse_rms(saved), final), q)
        saved_half = jnp.concatenate([saved_rows] + [swap_x(saved_rows, k, decoders) for k in range(1, NX)], axis=0)
        saved_half, b_near, c_far = lax.optimization_barrier((saved_half, b_near, c_far))
        saved_normed = jnp.concatenate([saved_half, swap_core(saved_half, decoders)], axis=0)
        k, v = mm(saved_normed, w_k).astype(bf16), mm(saved_normed, w_v).astype(bf16)
        c_near = swap_t(jnp.concatenate([fwd_shard, c_far], axis=1), 1, decoders)
        b_full = jnp.concatenate([b_pair, b_near], axis=1)
        dq, dk, dv = attend_back(q, k, v, b_full, w_o)
        dc = (mm_t(dk, w_k) + mm_t(dv, w_v)).astype(bf16)
        dn = mm_t(dq, w_q).astype(bf16)
        acc = dc[:half].astype(f32) + swap_core(dc[half:], decoders).astype(f32)
        acc16 = acc.astype(bf16)
        total = acc[:part]
        for k in range(1, NX):
            total = total + swap_x(acc16[k * part : (k + 1) * part], k, decoders).astype(f32)
        total, c_near = tie(total.astype(bf16), c_near)
        return fwd_shard, fwd_shard[:part], c_near, c_far, dn, total

    enc_y, top, near, c_far, dn, total = lax.cond(~dec, enc_phase1, dec_phase1, 0)

    arrivals = [
        move(total, lambda y, x, z, c, tt: (1, x, z, c, tt) if y == y_from else None) for y_from in (2, 3)
    ]
    dc_from2, dc_from3 = arrivals
    arrivals = [
        move(top, lambda y, x, z, c, tt: (y_to, x, z_to, c, tt) if y == 1 and z == 1 else None)
        for y_to in (2, 3)
        for z_to in (0, 1)
    ]
    top = sum(arrivals)

    def enc_phase2(_):
        b_full = jnp.concatenate([b_pair, near], axis=1)
        first_row = lambda y, z: y == 1
        dc_sum = dc_from2.astype(f32) + dc_from3.astype(f32)
        pair = dc_sum[:, : 2 * width] + swap_t(dc_sum[:, 2 * width :].astype(bf16), 1, first_row).astype(f32)
        mine = pair[:, :width] + swap_t(pair[:, width:].astype(bf16), 2, first_row).astype(f32)
        mine16 = mine.astype(bf16)
        mine = mine + move(
            mine16, lambda y, x, z, c, tt: (y, x, 1, c, tt) if y == 1 and z == 0 else None
        ).astype(f32)
        mine = mine.astype(bf16)
        pair = jnp.concatenate([mine, swap_t(mine, 2, top_row)], axis=1)
        u = jnp.concatenate([pair, swap_t(pair, 1, top_row)], axis=1)
        c_pair = jnp.concatenate([cot_shard, c_far], axis=1)
        c_pair, u = tie(c_pair, u)
        c_near = swap_t(c_pair, 1, encoders)
        u = final * u.astype(f32)
        r = inverse_rms(saved)
        block = (r * u - saved * r**3 * jnp.mean(u * saved, axis=-1, keepdims=True)).astype(bf16)
        slots = jnp.concatenate([block] + [swap_x(block, k, top_row) for k in range(1, NX)], axis=0)
        slots, c_near, y_out = lax.optimization_barrier((slots, c_near, enc_y))
        c_full = jnp.concatenate([c_pair, c_near], axis=1)
        swapped = swap_core(slots, top_row)
        pieces = []
        for xi in range(NX):
            k = xi ^ (NX - 1)
            pieces += [swapped[k * part : (k + 1) * part], slots[k * part : (k + 1) * part]]
        returned_full = jnp.concatenate(pieces, axis=0)
        sent = move(y_out, following(False))
        values = b_full.astype(f32)
        inverse = inverse_rms(values)
        normed = scale_rows(values, inverse, gain)
        q, k, v = project(normed, normed)
        upstream = jnp.where(last, returned_full, c_full)
        dq, dk, dv = attend_back(q, k, v, upstream, w_o)
        term = (mm_t(dq, w_q) + mm_t(dk, w_k) + mm_t(dv, w_v)).astype(bf16)
        term, sent = tie(term, sent)
        summed, row_sum = line_scatter(term, jnp.sum(gain * term.astype(f32) * values, axis=-1), encoders)
        return sent, summed, row_sum, inverse, upstream[:, :width]

    def dec_phase2(_):
        c_full = jnp.concatenate([fwd_shard, c_far, near], axis=1)
        all_top = jnp.concatenate([top, swap_t(top, 2, decoders)], axis=1)
        all_top = jnp.concatenate([all_top, swap_t(all_top, 1, decoders)], axis=1).astype(f32)
        row_part = jnp.sum(gain * dn.astype(f32) * a_values, axis=-1)
        dn_tied, all_top = tie(dn, all_top)
        dn_sum, row_sum = line_scatter(dn_tied, row_part, decoders)
        top_full = gather_rows(scale_rows(all_top, inverse_rms(all_top), final), decoders)
        values = c_full.astype(f32)
        normed = scale_rows(values, inverse_rms(values), gain)
        out = attend_out(*project(normed, top_full), w_o).astype(bf16)
        out, dn_sum = tie(out, dn_sum)
        summed, _ = line_scatter(out, None, decoders)
        dec_y = (fwd_shard.astype(f32) + summed).astype(bf16)
        return dec_y, dn_sum, row_sum, a_inverse, cot_shard

    sent, summed, row_sum, inverse, upstream = lax.cond(dec, dec_phase2, enc_phase2, 0)
    arrived = move(sent, following(True))
    from_enc = (~dec) & (section_index > 0)
    fwd_out = jnp.where(from_enc, sent, arrived)[None]
    grad_in = (
        upstream.astype(f32)
        + inverse * (gain[:, :width] * summed)
        - bwd_shard.astype(f32) * inverse**3 * (row_sum / full)
    ).astype(bf16)[None]
    return (fwd_out, grad_in)


def solution(mesh):
    in_specs = (
        P("section", None, "tensor"),
        P("section", None, "tensor"),
        P("section", None, "tensor"),
        P(None, "tensor"),
        P("section", "tensor"),
        P("tensor"),
        P("section", None, None, "tensor"),
        P("section", "tensor", None),
    )
    out_specs = (P("section", None, "tensor"), P("section", None, "tensor"))
    return jax.shard_map(body, mesh=mesh, in_specs=in_specs, out_specs=out_specs, check_vma=False)
```

```python
import jax
import jax.numpy as jnp
from jax import lax
from jax.sharding import PartitionSpec as P

HEAD_DIM = 256
NY, NX, NZ, NC, NT = 4, 4, 2, 2, 4
SECTION_COUNT = NY * NX * NZ * NC
ENC_SECTIONS = SECTION_COUNT // 2
LAST = ENC_SECTIONS - 1

epsilon = 1e-06
f32 = jnp.float32
bf16 = jnp.bfloat16

PLACES = [
    (y, x, z, c, t)
    for y in range(NY)
    for x in range(NX)
    for z in range(NZ)
    for c in range(NC)
    for t in range(NT)
]


def place_index(place):
    y, x, z, c, t = place
    return (((y * NX + x) * NZ + z) * NC + c) * NT + t


def section_of(place):
    return place_index(place) // NT


def move(value, route):
    pairs = []
    for place in PLACES:
        target = route(*place)
        if target is not None:
            pairs.append((place_index(place), place_index(target)))
    return lax.ppermute(value, ("section", "tensor"), pairs)


def is_dec(y):
    return y >= NY // 2


def everyone(y, z):
    return True


def encoders(y, z):
    return y < NY // 2


def decoders(y, z):
    return y >= NY // 2


def top_row(y, z):
    return y == 1 and z == 1


def swap_x(value, k, who):
    return move(value, lambda y, x, z, c, t: (y, x ^ k, z, c, t) if who(y, z) else None)


def swap_core(value, who):
    return move(value, lambda y, x, z, c, t: (y, x, z, 1 - c, t) if who(y, z) else None)


def swap_t(value, k, who):
    return move(value, lambda y, x, z, c, t: (y, x, z, c, t ^ k) if who(y, z) else None)


def after(value, *others):
    return lax.optimization_barrier((value,) + others)[0]


def tie(value, other):
    return lax.optimization_barrier((value, other))


def high_low(row_part, columns):
    high = row_part.astype(bf16)
    both = jnp.concatenate([high, (row_part - high.astype(f32)).astype(bf16)])
    spare = -both.shape[0] % columns
    return jnp.pad(both, (0, spare)).reshape(-1, columns)


def scatter_near(total, row_part, who):
    rows, half = total.shape[0], total.shape[1] // 2
    give = total[:, half:]
    if row_part is not None:
        give = jnp.concatenate([give, high_low(row_part, half)], axis=0)
    got = swap_t(give, 1, who).astype(f32)
    pair = total[:, :half].astype(f32) + got[:rows]
    if row_part is None:
        return pair, None
    tail = got[rows:].reshape(-1)
    return pair, row_part + tail[:rows] + tail[rows : 2 * rows]


def scatter_far(pair, sums, who, beside=None):
    rows, width = pair.shape[0], pair.shape[1] // 2
    give = pair[:, width:].astype(bf16)
    if sums is not None:
        give = jnp.concatenate([give, high_low(sums, width)], axis=0)
    if beside is not None:
        give, beside = tie(give, beside)
    got = swap_t(give, 2, who).astype(f32)
    summed = pair[:, :width] + got[:rows]
    if sums is not None:
        tail = got[rows:].reshape(-1)
        sums = (sums + tail[:rows] + tail[rows : 2 * rows]).reshape(rows, 1)
    return summed, sums, beside


def inverse_rms(values):
    return lax.rsqrt(jnp.mean(values * values, axis=-1, keepdims=True) + epsilon)


def scale_rows(values, inverse, gain_row):
    return (values * inverse * gain_row).astype(bf16)


def mm(a, b):
    return jnp.dot(a, b, preferred_element_type=f32)


def mm_t(a, b):
    return lax.dot_general(a, b, (((1,), (1,)), ((), ())), preferred_element_type=f32)


def t_mm(a, b):
    return lax.dot_general(a, b, (((0,), (0,)), ((), ())), preferred_element_type=f32)


def heads_of(matrix):
    return [matrix[:, h * HEAD_DIM : (h + 1) * HEAD_DIM] for h in range(matrix.shape[1] // HEAD_DIM)]


def softmax_rows(queries, keys):
    weights = jnp.exp(mm_t(queries, keys) * HEAD_DIM ** (-0.5))
    return weights / jnp.sum(weights, axis=-1, keepdims=True)


def attend_out(q, k, v, w_proj):
    mixed = [
        mm(softmax_rows(qh, kh).astype(bf16), vh).astype(bf16)
        for qh, kh, vh in zip(heads_of(q), heads_of(k), heads_of(v))
    ]
    return mm(jnp.concatenate(mixed, axis=1), w_proj)


def attend_back(q, k, v, upstream, w_proj):
    grad_mix = mm_t(upstream, w_proj).astype(bf16)
    dq, dk, dv = [], [], []
    for qh, kh, vh, gh in zip(heads_of(q), heads_of(k), heads_of(v), heads_of(grad_mix)):
        weights = softmax_rows(qh, kh)
        dv.append(t_mm(weights.astype(bf16), gh).astype(bf16))
        grad_weights = mm_t(gh, vh)
        grad_scores = (
            weights
            * (grad_weights - jnp.sum(weights * grad_weights, axis=-1, keepdims=True))
            * HEAD_DIM ** (-0.5)
        ).astype(bf16)
        dq.append(mm(grad_scores, kh).astype(bf16))
        dk.append(t_mm(grad_scores, qh).astype(bf16))
    return [jnp.concatenate(parts, axis=1) for parts in (dq, dk, dv)]


def gather_rows(own, who):
    half = jnp.concatenate([own] + [swap_x(own, k, who) for k in range(1, NX)], axis=0)
    return jnp.concatenate([half, swap_core(half, who)], axis=0)


def following(kind):
    def go(y, x, z, c, t):
        s = section_of((y, x, z, c, t))
        n = ((s + 1) % SECTION_COUNT) * NT + t
        return None if s == LAST or is_dec(y) != kind else PLACES[n]

    return go


def body(fwd_in, bwd_in, cotangent, enc_saved, norm_gain, final_gain, w_qkv, w_out):
    section_index = lax.axis_index("section")
    t = lax.axis_index("tensor")
    core = section_index % NC
    x_at = section_index // (NC * NZ) % NX
    dec = section_index >= ENC_SECTIONS
    last = section_index == LAST
    fwd_shard, bwd_shard, cot_shard = fwd_in[0], bwd_in[0], cotangent[0]
    rows, width = fwd_shard.shape
    full = width * NT
    part = rows // (NX * NC)
    half = rows // NC

    own_rows = lax.dynamic_slice_in_dim(enc_saved, (x_at * NC + core) * part, part, 0)
    a_shard = jnp.concatenate(
        [jnp.where(dec, bwd_shard, fwd_shard), own_rows, norm_gain, final_gain[None]], axis=0
    )
    b_shard = jnp.where(dec, cot_shard, bwd_shard)
    a_far = swap_t(a_shard, 2, everyone)
    a_pair = jnp.concatenate([a_shard, a_far], axis=1)
    b_far = swap_t(after(b_shard, a_far), 2, everyone)
    a_near = swap_t(a_pair, 1, everyone)
    b_pair = jnp.concatenate([b_shard, b_far], axis=1)
    a_all = jnp.concatenate([a_pair, a_near], axis=1)
    small = a_all[rows:].astype(f32)
    saved, gain, final = small[:part], small[part : part + 1], small[part + 1 :]

    order = [t, t ^ 2, t ^ 1, t ^ 3]
    w_in = w_qkv[0]
    turned = [lax.dynamic_slice_in_dim(w_in, o * width, width, 0) for o in order]
    w_q, w_k, w_v = (jnp.concatenate([w[:, i] for w in turned], axis=0) for i in range(3))
    w_o = jnp.concatenate([lax.dynamic_slice_in_dim(w_out[0], o * width, width, 1) for o in order], axis=1)

    a_values = a_all[:rows].astype(f32)
    a_inverse = inverse_rms(a_values)
    a_normed = scale_rows(a_values, a_inverse, gain)
    def project(normed, source):
        return mm(normed, w_q).astype(bf16), mm(source, w_k).astype(bf16), mm(source, w_v).astype(bf16)

    def enc_phase1(_):
        b_near = swap_t(b_pair, 1, encoders)
        out = attend_out(*project(a_normed, a_normed), w_o).astype(bf16)
        out, b_near = tie(out, b_near)
        summed, _, _ = scatter_far(*scatter_near(out, None, encoders), encoders)
        enc_y = (fwd_shard.astype(f32) + summed).astype(bf16)
        blocks = enc_y.reshape(NX, NC, part, width)
        passed, c_shard = tie(swap_core(blocks[:, 0], top_row), cot_shard)
        blocks = jnp.where(core == 1, blocks[:, 1], passed)
        c_far = swap_t(c_shard, 2, encoders)
        top = blocks[NX - 1]
        for k in range(1, NX):
            sent = move(
                blocks[(NX - 1) ^ k], lambda y, x, z, c, tt: (y, x ^ k, z, c, tt) if top_row(y, z) and x == NX - 1 else None
            )
            top = jnp.where(x_at ^ (NX - 1) == k, sent, top)
        return enc_y, top, b_near, c_far, out, out[:part, : 2 * width]

    def dec_phase1(_):
        b_near = swap_t(b_pair, 1, decoders)
        c_far = swap_t(fwd_shard, 2, decoders)
        q = mm(a_normed, w_q).astype(bf16)
        saved_rows, q = tie(scale_rows(saved, inverse_rms(saved), final), q)
        saved_half = jnp.concatenate([saved_rows] + [swap_x(saved_rows, k, decoders) for k in range(1, NX)], axis=0)
        saved_half, b_near, c_far = lax.optimization_barrier((saved_half, b_near, c_far))
        saved_normed = jnp.concatenate([saved_half, swap_core(saved_half, decoders)], axis=0)
        k, v = mm(saved_normed, w_k).astype(bf16), mm(saved_normed, w_v).astype(bf16)
        c_near = swap_t(jnp.concatenate([fwd_shard, c_far], axis=1), 1, decoders)
        b_full = jnp.concatenate([b_pair, b_near], axis=1)
        dq, dk, dv = attend_back(q, k, v, b_full, w_o)
        dc = (mm_t(dk, w_k) + mm_t(dv, w_v)).astype(bf16)
        dn = mm_t(dq, w_q).astype(bf16)
        acc = dc[:half].astype(f32) + swap_core(dc[half:], decoders).astype(f32)
        acc16 = acc.astype(bf16)
        total = acc[:part]
        for k in range(1, NX):
            total = total + swap_x(acc16[k * part : (k + 1) * part], k, decoders).astype(f32)
        total, c_near = tie(total, c_near)
        total = total[:, : 2 * width] + swap_t(total[:, 2 * width :].astype(bf16), 1, decoders).astype(f32)
        total = total.astype(bf16)
        return fwd_shard, fwd_shard[:part], c_near, c_far, dn, total

    enc_y, top, near, c_far, dn, total = lax.cond(~dec, enc_phase1, dec_phase1, 0)

    arrivals = [
        move(total, lambda y, x, z, c, tt: (1, x, z, c, tt) if y == y_from else None) for y_from in (2, 3)
    ]
    dc_from2, dc_from3 = arrivals
    arrivals = [
        move(top, lambda y, x, z, c, tt: (y_to, x, z_to, c, tt) if y == 1 and z == 1 else None)
        for y_to in (2, 3)
        for z_to in (0, 1)
    ]
    top = sum(arrivals)

    def enc_phase2(_):
        b_full = jnp.concatenate([b_pair, near], axis=1)
        first_row = lambda y, z: y == 1
        pair = dc_from2.astype(f32) + dc_from3.astype(f32)
        mine = pair[:, :width] + swap_t(pair[:, width:].astype(bf16), 2, first_row).astype(f32)
        mine16 = mine.astype(bf16)
        mine = mine + move(
            mine16, lambda y, x, z, c, tt: (y, x, 1, c, tt) if y == 1 and z == 0 else None
        ).astype(f32)
        mine = mine.astype(bf16)
        pair = jnp.concatenate([mine, swap_t(mine, 2, top_row)], axis=1)
        u = jnp.concatenate([pair, swap_t(pair, 1, top_row)], axis=1)
        c_pair = jnp.concatenate([cot_shard, c_far], axis=1)
        c_pair, u, y_out = lax.optimization_barrier((c_pair, u, enc_y))
        c_near = swap_t(c_pair, 1, encoders)
        u = final * u.astype(f32)
        r = inverse_rms(saved)
        block = (r * u - saved * r**3 * jnp.mean(u * saved, axis=-1, keepdims=True)).astype(bf16)
        slots = [block]
        for k in range(1, NX):
            slots.append(
                move(block, lambda y, x, z, c, tt: (y, NX - 1, z, c, tt) if top_row(y, z) and x ^ k == NX - 1 else None)
            )
        slots = jnp.concatenate(slots, axis=0)
        slots, c_near = tie(slots, c_near)
        c_full = jnp.concatenate([c_pair, c_near], axis=1)
        swapped = swap_core(slots, top_row)
        pieces = []
        for xi in range(NX):
            k = xi ^ (NX - 1)
            pieces += [swapped[k * part : (k + 1) * part], slots[k * part : (k + 1) * part]]
        returned_full = jnp.concatenate(pieces, axis=0)
        sent = move(y_out, following(False))
        values = b_full.astype(f32)
        inverse = inverse_rms(values)
        normed = scale_rows(values, inverse, gain)
        q, k, v = project(normed, normed)
        upstream = jnp.where(last, returned_full, c_full)
        dq, dk, dv = attend_back(q, k, v, upstream, w_o)
        term = (mm_t(dq, w_q) + mm_t(dk, w_k) + mm_t(dv, w_v)).astype(bf16)
        term, sent = tie(term, sent)
        near_half = scatter_near(term, jnp.sum(gain * term.astype(f32) * values, axis=-1), encoders)
        summed, row_sum, _ = scatter_far(*near_half, encoders)
        return sent, summed, row_sum, inverse, upstream[:, :width]

    def dec_phase2(_):
        c_full = jnp.concatenate([fwd_shard, c_far, near], axis=1)
        all_top = jnp.concatenate([top, swap_t(top, 2, decoders)], axis=1)
        all_top = jnp.concatenate([all_top, swap_t(all_top, 1, decoders)], axis=1).astype(f32)
        row_part = jnp.sum(gain * dn.astype(f32) * a_values, axis=-1)
        dn_tied, all_top = tie(dn, all_top)
        dn_pair, row_part = scatter_near(dn_tied, row_part, decoders)
        top_full = gather_rows(scale_rows(all_top, inverse_rms(all_top), final), decoders)
        values = c_full.astype(f32)
        normed = scale_rows(values, inverse_rms(values), gain)
        out = attend_out(*project(normed, top_full), w_o).astype(bf16)
        dn_sum, row_sum, out = scatter_far(dn_pair, row_part, decoders, out)
        out_pair, _ = scatter_near(out, None, decoders)
        summed, _, dn_sum = scatter_far(out_pair, None, decoders, dn_sum)
        dec_y = (fwd_shard.astype(f32) + summed).astype(bf16)
        return dec_y, dn_sum, row_sum, a_inverse, cot_shard

    sent, summed, row_sum, inverse, upstream = lax.cond(dec, dec_phase2, enc_phase2, 0)
    arrived = move(sent, following(True))
    from_enc = (~dec) & (section_index > 0)
    fwd_out = jnp.where(from_enc, sent, arrived)[None]
    grad_in = (
        upstream.astype(f32)
        + inverse * (gain[:, :width] * summed)
        - bwd_shard.astype(f32) * inverse**3 * (row_sum / full)
    ).astype(bf16)[None]
    return (fwd_out, grad_in)


def solution(mesh):
    in_specs = (
        P("section", None, "tensor"),
        P("section", None, "tensor"),
        P("section", None, "tensor"),
        P(None, "tensor"),
        P("section", "tensor"),
        P("tensor"),
        P("section", None, None, "tensor"),
        P("section", "tensor", None),
    )
    out_specs = (P("section", None, "tensor"), P("section", None, "tensor"))
    return jax.shard_map(body, mesh=mesh, in_specs=in_specs, out_specs=out_specs, check_vma=False)
```

```python
import jax
import jax.numpy as jnp
from jax import lax
from jax.sharding import PartitionSpec as P

HEAD_DIM = 256
NY, NX, NZ, NC, NT = 4, 4, 2, 2, 4
SECTION_COUNT = NY * NX * NZ * NC
ENC_SECTIONS = SECTION_COUNT // 2
LAST = ENC_SECTIONS - 1

epsilon = 1e-06
f32 = jnp.float32
bf16 = jnp.bfloat16

PLACES = [
    (y, x, z, c, t)
    for y in range(NY)
    for x in range(NX)
    for z in range(NZ)
    for c in range(NC)
    for t in range(NT)
]


def place_index(place):
    y, x, z, c, t = place
    return (((y * NX + x) * NZ + z) * NC + c) * NT + t


def section_of(place):
    return place_index(place) // NT


def move(value, route):
    pairs = []
    for place in PLACES:
        target = route(*place)
        if target is not None:
            pairs.append((place_index(place), place_index(target)))
    return lax.ppermute(value, ("section", "tensor"), pairs)


def is_dec(y):
    return y >= NY // 2


def everyone(y, z):
    return True


def encoders(y, z):
    return y < NY // 2


def decoders(y, z):
    return y >= NY // 2


def top_row(y, z):
    return y == 1 and z == 1


def swap_x(value, k, who):
    return move(value, lambda y, x, z, c, t: (y, x ^ k, z, c, t) if who(y, z) else None)


def swap_core(value, who):
    return move(value, lambda y, x, z, c, t: (y, x, z, 1 - c, t) if who(y, z) else None)


def swap_t(value, k, who):
    return move(value, lambda y, x, z, c, t: (y, x, z, c, t ^ k) if who(y, z) else None)


def after(value, *others):
    return lax.optimization_barrier((value,) + others)[0]


def tie(value, other):
    return lax.optimization_barrier((value, other))


def high_low(row_part, columns):
    high = row_part.astype(bf16)
    both = jnp.concatenate([high, (row_part - high.astype(f32)).astype(bf16)])
    spare = -both.shape[0] % columns
    return jnp.pad(both, (0, spare)).reshape(-1, columns)


def scatter_near(total, row_part, who):
    rows, half = total.shape[0], total.shape[1] // 2
    give = total[:, half:]
    if row_part is not None:
        give = jnp.concatenate([give, high_low(row_part, half)], axis=0)
    got = swap_t(give, 1, who).astype(f32)
    pair = total[:, :half].astype(f32) + got[:rows]
    if row_part is None:
        return pair, None
    tail = got[rows:].reshape(-1)
    return pair, row_part + tail[:rows] + tail[rows : 2 * rows]


def scatter_far(pair, sums, who, beside=None):
    rows, width = pair.shape[0], pair.shape[1] // 2
    give = pair[:, width:].astype(bf16)
    if sums is not None:
        give = jnp.concatenate([give, high_low(sums, width)], axis=0)
    if beside is not None:
        give, beside = tie(give, beside)
    got = swap_t(give, 2, who).astype(f32)
    summed = pair[:, :width] + got[:rows]
    if sums is not None:
        tail = got[rows:].reshape(-1)
        sums = (sums + tail[:rows] + tail[rows : 2 * rows]).reshape(rows, 1)
    return summed, sums, beside


def scatter(total, row_part, who, beside=None):
    rows, width = total.shape[0], total.shape[1] // NT
    give3 = total[:, 3 * width :]
    if row_part is not None:
        give3 = jnp.concatenate([give3, high_low(row_part, width)], axis=0)
    give1, got3 = tie(total[:, 2 * width : 3 * width], swap_t(give3, 1, who))
    got3 = got3.astype(f32)
    give2 = (total[:, width : 2 * width].astype(f32) + got3[:rows]).astype(bf16)
    if row_part is not None:
        tail = got3[rows:].reshape(-1)
        row_part = row_part + tail[:rows] + tail[rows : 2 * rows]
        give2 = jnp.concatenate([give2, high_low(row_part, width)], axis=0)
    if beside is not None:
        give2, beside = tie(give2, beside)
    got2 = swap_t(give2, 2, who).astype(f32)
    got1 = swap_t(give1, 1, who).astype(f32)
    summed = total[:, :width].astype(f32) + got1 + got2[:rows]
    if row_part is not None:
        tail = got2[rows:].reshape(-1)
        row_part = (row_part + tail[:rows] + tail[rows : 2 * rows]).reshape(rows, 1)
    return summed, row_part, beside


def inverse_rms(values):
    return lax.rsqrt(jnp.mean(values * values, axis=-1, keepdims=True) + epsilon)


def scale_rows(values, inverse, gain_row):
    return (values * inverse * gain_row).astype(bf16)


def mm(a, b):
    return jnp.dot(a, b, preferred_element_type=f32)


def mm_t(a, b):
    return lax.dot_general(a, b, (((1,), (1,)), ((), ())), preferred_element_type=f32)


def t_mm(a, b):
    return lax.dot_general(a, b, (((0,), (0,)), ((), ())), preferred_element_type=f32)


def heads_of(matrix):
    return [matrix[:, h * HEAD_DIM : (h + 1) * HEAD_DIM] for h in range(matrix.shape[1] // HEAD_DIM)]


def softmax_rows(queries, keys):
    weights = jnp.exp(mm_t(queries, keys) * HEAD_DIM ** (-0.5))
    return weights / jnp.sum(weights, axis=-1, keepdims=True)


def attend_out(q, k, v, w_proj):
    mixed = [
        mm(softmax_rows(qh, kh).astype(bf16), vh).astype(bf16)
        for qh, kh, vh in zip(heads_of(q), heads_of(k), heads_of(v))
    ]
    return mm(jnp.concatenate(mixed, axis=1), w_proj)


def attend_back(q, k, v, upstream, w_proj):
    grad_mix = mm_t(upstream, w_proj).astype(bf16)
    dq, dk, dv = [], [], []
    for qh, kh, vh, gh in zip(heads_of(q), heads_of(k), heads_of(v), heads_of(grad_mix)):
        weights = softmax_rows(qh, kh)
        dv.append(t_mm(weights.astype(bf16), gh).astype(bf16))
        grad_weights = mm_t(gh, vh)
        grad_scores = (
            weights
            * (grad_weights - jnp.sum(weights * grad_weights, axis=-1, keepdims=True))
            * HEAD_DIM ** (-0.5)
        ).astype(bf16)
        dq.append(mm(grad_scores, kh).astype(bf16))
        dk.append(t_mm(grad_scores, qh).astype(bf16))
    return [jnp.concatenate(parts, axis=1) for parts in (dq, dk, dv)]


def gather_rows(own, who):
    half = jnp.concatenate([own] + [swap_x(own, k, who) for k in range(1, NX)], axis=0)
    return jnp.concatenate([half, swap_core(half, who)], axis=0)


def following(kind):
    def go(y, x, z, c, t):
        s = section_of((y, x, z, c, t))
        n = ((s + 1) % SECTION_COUNT) * NT + t
        return None if s == LAST or is_dec(y) != kind else PLACES[n]

    return go


def body(fwd_in, bwd_in, cotangent, enc_saved, norm_gain, final_gain, w_qkv, w_out):
    section_index = lax.axis_index("section")
    t = lax.axis_index("tensor")
    core = section_index % NC
    x_at = section_index // (NC * NZ) % NX
    dec = section_index >= ENC_SECTIONS
    last = section_index == LAST
    fwd_shard, bwd_shard, cot_shard = fwd_in[0], bwd_in[0], cotangent[0]
    rows, width = fwd_shard.shape
    full = width * NT
    part = rows // (NX * NC)
    half = rows // NC

    own_rows = lax.dynamic_slice_in_dim(enc_saved, (x_at * NC + core) * part, part, 0)
    a_shard = jnp.concatenate(
        [jnp.where(dec, bwd_shard, fwd_shard), own_rows, norm_gain, final_gain[None]], axis=0
    )
    b_shard = jnp.where(dec, cot_shard, bwd_shard)
    a_far = swap_t(a_shard, 2, everyone)
    a_near = swap_t(a_shard, 1, everyone)
    a_last = swap_t(a_far, 1, everyone)
    b_far = swap_t(after(b_shard, a_far), 2, everyone)
    b_own, a_near = tie(b_shard, a_near)
    b_near = swap_t(b_own, 1, everyone)
    a_all = jnp.concatenate([a_shard, a_far, a_near, a_last], axis=1)
    b_three = jnp.concatenate([b_shard, b_far, b_near], axis=1)

    small = a_all[rows:].astype(f32)
    saved, gain, final = small[:part], small[part : part + 1], small[part + 1 :]

    order = [t, t ^ 2, t ^ 1, t ^ 3]
    w_in = w_qkv[0]
    turned = [lax.dynamic_slice_in_dim(w_in, o * width, width, 0) for o in order]
    w_q, w_k, w_v = (jnp.concatenate([w[:, i] for w in turned], axis=0) for i in range(3))
    w_o = jnp.concatenate([lax.dynamic_slice_in_dim(w_out[0], o * width, width, 1) for o in order], axis=1)

    a_values = a_all[:rows].astype(f32)
    a_inverse = inverse_rms(a_values)
    a_normed = scale_rows(a_values, a_inverse, gain)
    def project(normed, source):
        return mm(normed, w_q).astype(bf16), mm(source, w_k).astype(bf16), mm(source, w_v).astype(bf16)

    def enc_phase1(_):
        b_last = swap_t(b_far, 1, encoders)
        out = attend_out(*project(a_normed, a_normed), w_o).astype(bf16)
        out, b_last = tie(out, b_last)
        summed, _, _ = scatter(out, None, encoders)
        enc_y = (fwd_shard.astype(f32) + summed).astype(bf16)
        blocks = enc_y.reshape(NX, NC, part, width)
        passed, c_shard = tie(swap_core(blocks[:, 0], top_row), cot_shard)
        blocks = jnp.where(core == 1, blocks[:, 1], passed)
        c_far = swap_t(c_shard, 2, encoders)
        top = blocks[NX - 1]
        for k in range(1, NX):
            sent = move(
                blocks[(NX - 1) ^ k], lambda y, x, z, c, tt: (y, x ^ k, z, c, tt) if top_row(y, z) and x == NX - 1 else None
            )
            top = jnp.where(x_at ^ (NX - 1) == k, sent, top)
        return enc_y, top, jnp.concatenate([b_last, b_last], axis=1), c_far, out, out[:part, : 2 * width]

    def dec_phase1(_):
        b_last = swap_t(b_far, 1, decoders)
        c_far = swap_t(fwd_shard, 2, decoders)
        q = mm(a_normed, w_q).astype(bf16)
        saved_rows, q = tie(scale_rows(saved, inverse_rms(saved), final), q)
        saved_half = jnp.concatenate([saved_rows] + [swap_x(saved_rows, k, decoders) for k in range(1, NX)], axis=0)
        saved_half, b_last, c_far = lax.optimization_barrier((saved_half, b_last, c_far))
        saved_normed = jnp.concatenate([saved_half, swap_core(saved_half, decoders)], axis=0)
        k, v = mm(saved_normed, w_k).astype(bf16), mm(saved_normed, w_v).astype(bf16)
        c_near = swap_t(jnp.concatenate([fwd_shard, c_far], axis=1), 1, decoders)
        b_full = jnp.concatenate([b_three, b_last], axis=1)
        dq, dk, dv = attend_back(q, k, v, b_full, w_o)
        dc = (mm_t(dk, w_k) + mm_t(dv, w_v)).astype(bf16)
        dn = mm_t(dq, w_q).astype(bf16)
        acc = dc[:half].astype(f32) + swap_core(dc[half:], decoders).astype(f32)
        acc16 = acc.astype(bf16)
        total = acc[:part]
        for k in range(1, NX):
            total = total + swap_x(acc16[k * part : (k + 1) * part], k, decoders).astype(f32)
        total, c_near = tie(total, c_near)
        total = total[:, : 2 * width] + swap_t(total[:, 2 * width :].astype(bf16), 1, decoders).astype(f32)
        total = total.astype(bf16)
        return fwd_shard, fwd_shard[:part], c_near, c_far, dn, total

    enc_y, top, near, c_far, dn, total = lax.cond(~dec, enc_phase1, dec_phase1, 0)

    arrivals = [
        move(total, lambda y, x, z, c, tt: (1, x, z, c, tt) if y == y_from else None) for y_from in (2, 3)
    ]
    dc_from2, dc_from3 = arrivals
    arrivals = [
        move(top, lambda y, x, z, c, tt: (y_to, x, z_to, c, tt) if y == 1 and z == 1 else None)
        for y_to in (2, 3)
        for z_to in (0, 1)
    ]
    top = sum(arrivals)

    def enc_phase2(_):
        b_full = jnp.concatenate([b_three, near[:, :width]], axis=1)
        first_row = lambda y, z: y == 1
        pair = dc_from2.astype(f32) + dc_from3.astype(f32)
        mine = pair[:, :width] + swap_t(pair[:, width:].astype(bf16), 2, first_row).astype(f32)
        mine16 = mine.astype(bf16)
        mine = mine + move(
            mine16, lambda y, x, z, c, tt: (y, x, 1, c, tt) if y == 1 and z == 0 else None
        ).astype(f32)
        mine = mine.astype(bf16)
        pair = jnp.concatenate([mine, swap_t(mine, 2, top_row)], axis=1)
        u = jnp.concatenate([pair, swap_t(pair, 1, top_row)], axis=1)
        c_pair = jnp.concatenate([cot_shard, c_far], axis=1)
        c_pair, u, y_out = lax.optimization_barrier((c_pair, u, enc_y))
        c_near = swap_t(c_pair, 1, encoders)
        u = final * u.astype(f32)
        r = inverse_rms(saved)
        block = (r * u - saved * r**3 * jnp.mean(u * saved, axis=-1, keepdims=True)).astype(bf16)
        slots = [block]
        for k in range(1, NX):
            slots.append(
                move(block, lambda y, x, z, c, tt: (y, NX - 1, z, c, tt) if top_row(y, z) and x ^ k == NX - 1 else None)
            )
        slots = jnp.concatenate(slots, axis=0)
        slots, c_near = tie(slots, c_near)
        c_full = jnp.concatenate([c_pair, c_near], axis=1)
        swapped = swap_core(slots, top_row)
        pieces = []
        for xi in range(NX):
            k = xi ^ (NX - 1)
            pieces += [swapped[k * part : (k + 1) * part], slots[k * part : (k + 1) * part]]
        returned_full = jnp.concatenate(pieces, axis=0)
        sent = move(y_out, following(False))
        values = b_full.astype(f32)
        inverse = inverse_rms(values)
        normed = scale_rows(values, inverse, gain)
        q, k, v = project(normed, normed)
        upstream = jnp.where(last, returned_full, c_full)
        dq, dk, dv = attend_back(q, k, v, upstream, w_o)
        term = (mm_t(dq, w_q) + mm_t(dk, w_k) + mm_t(dv, w_v)).astype(bf16)
        term, sent = tie(term, sent)
        summed, row_sum, _ = scatter(term, jnp.sum(gain * term.astype(f32) * values, axis=-1), encoders)
        return sent, summed, row_sum, inverse, upstream[:, :width]

    def dec_phase2(_):
        c_full = jnp.concatenate([fwd_shard, c_far, near], axis=1)
        all_top = jnp.concatenate([top, swap_t(top, 2, decoders)], axis=1)
        all_top = jnp.concatenate([all_top, swap_t(all_top, 1, decoders)], axis=1).astype(f32)
        row_part = jnp.sum(gain * dn.astype(f32) * a_values, axis=-1)
        dn_tied, all_top = tie(dn, all_top)
        dn_pair, row_part = scatter_near(dn_tied, row_part, decoders)
        top_full = gather_rows(scale_rows(all_top, inverse_rms(all_top), final), decoders)
        values = c_full.astype(f32)
        normed = scale_rows(values, inverse_rms(values), gain)
        out = attend_out(*project(normed, top_full), w_o).astype(bf16)
        dn_sum, row_sum, out = scatter_far(dn_pair, row_part, decoders, out)
        summed, _, dn_sum = scatter(out, None, decoders, dn_sum)
        dec_y = (fwd_shard.astype(f32) + summed).astype(bf16)
        return dec_y, dn_sum, row_sum, a_inverse, cot_shard

    sent, summed, row_sum, inverse, upstream = lax.cond(dec, dec_phase2, enc_phase2, 0)
    arrived = move(sent, following(True))
    from_enc = (~dec) & (section_index > 0)
    fwd_out = jnp.where(from_enc, sent, arrived)[None]
    grad_in = (
        upstream.astype(f32)
        + inverse * (gain[:, :width] * summed)
        - bwd_shard.astype(f32) * inverse**3 * (row_sum / full)
    ).astype(bf16)[None]
    return (fwd_out, grad_in)


def solution(mesh):
    in_specs = (
        P("section", None, "tensor"),
        P("section", None, "tensor"),
        P("section", None, "tensor"),
        P(None, "tensor"),
        P("section", "tensor"),
        P("tensor"),
        P("section", None, None, "tensor"),
        P("section", "tensor", None),
    )
    out_specs = (P("section", None, "tensor"), P("section", None, "tensor"))
    return jax.shard_map(body, mesh=mesh, in_specs=in_specs, out_specs=out_specs, check_vma=False)
```

```python
import jax
import jax.numpy as jnp
from jax import lax
from jax.sharding import PartitionSpec as P

HEAD_DIM = 256
NY, NX, NZ, NC, NT = 4, 4, 2, 2, 4
SECTION_COUNT = NY * NX * NZ * NC
ENC_SECTIONS = SECTION_COUNT // 2
LAST = ENC_SECTIONS - 1

epsilon = 1e-06
f32 = jnp.float32
bf16 = jnp.bfloat16

PLACES = [
    (y, x, z, c, t)
    for y in range(NY)
    for x in range(NX)
    for z in range(NZ)
    for c in range(NC)
    for t in range(NT)
]


def place_index(place):
    y, x, z, c, t = place
    return (((y * NX + x) * NZ + z) * NC + c) * NT + t


def section_of(place):
    return place_index(place) // NT


def move(value, route):
    pairs = []
    for place in PLACES:
        target = route(*place)
        if target is not None:
            pairs.append((place_index(place), place_index(target)))
    return lax.ppermute(value, ("section", "tensor"), pairs)


def is_dec(y):
    return y >= NY // 2


def everyone(y, z):
    return True


def encoders(y, z):
    return y < NY // 2


def decoders(y, z):
    return y >= NY // 2


def top_row(y, z):
    return y == 1 and z == 1


def swap_x(value, k, who):
    return move(value, lambda y, x, z, c, t: (y, x ^ k, z, c, t) if who(y, z) else None)


def swap_core(value, who):
    return move(value, lambda y, x, z, c, t: (y, x, z, 1 - c, t) if who(y, z) else None)


def swap_t(value, k, who):
    return move(value, lambda y, x, z, c, t: (y, x, z, c, t ^ k) if who(y, z) else None)


def after(value, *others):
    return lax.optimization_barrier((value,) + others)[0]


def tie(value, other):
    return lax.optimization_barrier((value, other))


def high_low(row_part, columns):
    high = row_part.astype(bf16)
    both = jnp.concatenate([high, (row_part - high.astype(f32)).astype(bf16)])
    spare = -both.shape[0] % columns
    return jnp.pad(both, (0, spare)).reshape(-1, columns)


def scatter_near(total, row_part, who):
    rows, half = total.shape[0], total.shape[1] // 2
    give = total[:, half:]
    if row_part is not None:
        give = jnp.concatenate([give, high_low(row_part, half)], axis=0)
    got = swap_t(give, 1, who).astype(f32)
    pair = total[:, :half].astype(f32) + got[:rows]
    if row_part is None:
        return pair, None
    tail = got[rows:].reshape(-1)
    return pair, row_part + tail[:rows] + tail[rows : 2 * rows]


def scatter_far(pair, sums, who, beside=None):
    rows, width = pair.shape[0], pair.shape[1] // 2
    give = pair[:, width:].astype(bf16)
    if sums is not None:
        give = jnp.concatenate([give, high_low(sums, width)], axis=0)
    if beside is not None:
        give, beside = tie(give, beside)
    got = swap_t(give, 2, who).astype(f32)
    summed = pair[:, :width] + got[:rows]
    if sums is not None:
        tail = got[rows:].reshape(-1)
        sums = (sums + tail[:rows] + tail[rows : 2 * rows]).reshape(rows, 1)
    return summed, sums, beside


def scatter(total, row_part, who, beside=None):
    rows, width = total.shape[0], total.shape[1] // NT
    give3 = total[:, 3 * width :]
    if row_part is not None:
        give3 = jnp.concatenate([give3, high_low(row_part, width)], axis=0)
    give1, got3 = tie(total[:, 2 * width : 3 * width], swap_t(give3, 1, who))
    got3 = got3.astype(f32)
    give2 = (total[:, width : 2 * width].astype(f32) + got3[:rows]).astype(bf16)
    if row_part is not None:
        tail = got3[rows:].reshape(-1)
        row_part = row_part + tail[:rows] + tail[rows : 2 * rows]
        give2 = jnp.concatenate([give2, high_low(row_part, width)], axis=0)
    if beside is not None:
        give2, beside = tie(give2, beside)
    got2 = swap_t(give2, 2, who).astype(f32)
    got1 = swap_t(give1, 1, who).astype(f32)
    summed = total[:, :width].astype(f32) + got1 + got2[:rows]
    if row_part is not None:
        tail = got2[rows:].reshape(-1)
        row_part = (row_part + tail[:rows] + tail[rows : 2 * rows]).reshape(rows, 1)
    return summed, row_part, beside


def inverse_rms(values):
    return lax.rsqrt(jnp.mean(values * values, axis=-1, keepdims=True) + epsilon)


def scale_rows(values, inverse, gain_row):
    return (values * inverse * gain_row).astype(bf16)


def mm(a, b):
    return jnp.dot(a, b, preferred_element_type=f32)


def mm_t(a, b):
    return lax.dot_general(a, b, (((1,), (1,)), ((), ())), preferred_element_type=f32)


def t_mm(a, b):
    return lax.dot_general(a, b, (((0,), (0,)), ((), ())), preferred_element_type=f32)


def heads_of(matrix):
    return [matrix[:, h * HEAD_DIM : (h + 1) * HEAD_DIM] for h in range(matrix.shape[1] // HEAD_DIM)]


def softmax_rows(queries, keys):
    weights = jnp.exp(mm_t(queries, keys) * HEAD_DIM ** (-0.5))
    return weights / jnp.sum(weights, axis=-1, keepdims=True)


def attend_out(q, k, v, w_proj):
    mixed = [
        mm(softmax_rows(qh, kh).astype(bf16), vh).astype(bf16)
        for qh, kh, vh in zip(heads_of(q), heads_of(k), heads_of(v))
    ]
    return mm(jnp.concatenate(mixed, axis=1), w_proj)


def attend_back(q, k, v, upstream, w_proj):
    grad_mix = mm_t(upstream, w_proj).astype(bf16)
    dq, dk, dv = [], [], []
    for qh, kh, vh, gh in zip(heads_of(q), heads_of(k), heads_of(v), heads_of(grad_mix)):
        weights = softmax_rows(qh, kh)
        dv.append(t_mm(weights.astype(bf16), gh).astype(bf16))
        grad_weights = mm_t(gh, vh)
        grad_scores = (
            weights
            * (grad_weights - jnp.sum(weights * grad_weights, axis=-1, keepdims=True))
            * HEAD_DIM ** (-0.5)
        ).astype(bf16)
        dq.append(mm(grad_scores, kh).astype(bf16))
        dk.append(t_mm(grad_scores, qh).astype(bf16))
    return [jnp.concatenate(parts, axis=1) for parts in (dq, dk, dv)]


def gather_rows(own, who):
    half = jnp.concatenate([own] + [swap_x(own, k, who) for k in range(1, NX)], axis=0)
    return jnp.concatenate([half, swap_core(half, who)], axis=0)


def following(kind):
    def go(y, x, z, c, t):
        s = section_of((y, x, z, c, t))
        n = ((s + 1) % SECTION_COUNT) * NT + t
        return None if s == LAST or is_dec(y) != kind else PLACES[n]

    return go


def body(fwd_in, bwd_in, cotangent, enc_saved, norm_gain, final_gain, w_qkv, w_out):
    section_index = lax.axis_index("section")
    t = lax.axis_index("tensor")
    core = section_index % NC
    x_at = section_index // (NC * NZ) % NX
    dec = section_index >= ENC_SECTIONS
    last = section_index == LAST
    fwd_shard, bwd_shard, cot_shard = fwd_in[0], bwd_in[0], cotangent[0]
    rows, width = fwd_shard.shape
    full = width * NT
    part = rows // (NX * NC)
    half = rows // NC

    own_rows = lax.dynamic_slice_in_dim(enc_saved, (x_at * NC + core) * part, part, 0)
    a_shard = jnp.concatenate(
        [jnp.where(dec, bwd_shard, fwd_shard), own_rows, norm_gain, final_gain[None]], axis=0
    )
    b_shard = jnp.where(dec, cot_shard, bwd_shard)
    a_far = swap_t(a_shard, 2, everyone)
    a_near = swap_t(a_shard, 1, everyone)
    a_last = swap_t(a_far, 1, everyone)
    b_far = swap_t(after(b_shard, a_far), 2, everyone)
    b_own, a_near = tie(b_shard, a_near)
    b_near = swap_t(b_own, 1, everyone)
    a_all = jnp.concatenate([a_shard, a_far, a_near, a_last], axis=1)
    b_three = jnp.concatenate([b_shard, b_far, b_near], axis=1)

    small = a_all[rows:].astype(f32)
    saved, gain, final = small[:part], small[part : part + 1], small[part + 1 :]

    order = [t, t ^ 2, t ^ 1, t ^ 3]
    w_in = w_qkv[0]
    turned = [lax.dynamic_slice_in_dim(w_in, o * width, width, 0) for o in order]
    w_q, w_k, w_v = (jnp.concatenate([w[:, i] for w in turned], axis=0) for i in range(3))
    w_o = jnp.concatenate([lax.dynamic_slice_in_dim(w_out[0], o * width, width, 1) for o in order], axis=1)

    a_values = a_all[:rows].astype(f32)
    a_inverse = inverse_rms(a_values)
    a_normed = scale_rows(a_values, a_inverse, gain)
    def project(normed, source):
        return mm(normed, w_q).astype(bf16), mm(source, w_k).astype(bf16), mm(source, w_v).astype(bf16)

    def enc_phase1(_):
        b_last = swap_t(b_far, 1, encoders)
        out = attend_out(*project(a_normed, a_normed), w_o).astype(bf16)
        out, b_last = tie(out, b_last)
        summed, _, _ = scatter(out, None, encoders)
        enc_y = (fwd_shard.astype(f32) + summed).astype(bf16)
        blocks = enc_y.reshape(NX, NC, part, width)
        passed, c_shard = tie(swap_core(blocks[:, 0], top_row), cot_shard)
        blocks = jnp.where(core == 1, blocks[:, 1], passed)
        c_far = swap_t(c_shard, 2, encoders)
        top = blocks[NX - 1]
        for k in range(1, NX):
            sent = move(
                blocks[(NX - 1) ^ k], lambda y, x, z, c, tt: (y, x ^ k, z, c, tt) if top_row(y, z) and x == NX - 1 else None
            )
            top = jnp.where(x_at ^ (NX - 1) == k, sent, top)
        return enc_y, top, jnp.concatenate([b_last, b_last], axis=1), c_far, out, out[:part, : 2 * width]

    def dec_phase1(_):
        b_last = swap_t(b_far, 1, decoders)
        q = mm(a_normed, w_q).astype(bf16)
        saved_rows, q = tie(scale_rows(saved, inverse_rms(saved), final), q)
        saved_half = jnp.concatenate([saved_rows] + [swap_x(saved_rows, k, decoders) for k in range(1, NX)], axis=0)
        saved_half, b_last = tie(saved_half, b_last)
        saved_normed = jnp.concatenate([saved_half, swap_core(saved_half, decoders)], axis=0)
        k, v = mm(saved_normed, w_k).astype(bf16), mm(saved_normed, w_v).astype(bf16)
        c_shard, b_last = tie(fwd_shard, b_last)
        c_far, c_near = swap_t(c_shard, 2, decoders), swap_t(c_shard, 1, decoders)
        b_full = jnp.concatenate([b_three, b_last], axis=1)
        dq, dk, dv = attend_back(q, k, v, b_full, w_o)
        dc = (mm_t(dk, w_k) + mm_t(dv, w_v)).astype(bf16)
        dn = mm_t(dq, w_q).astype(bf16)
        acc = dc[:half].astype(f32) + swap_core(dc[half:], decoders).astype(f32)
        acc16 = acc.astype(bf16)
        total = acc[:part]
        for k in range(1, NX):
            total = total + swap_x(acc16[k * part : (k + 1) * part], k, decoders).astype(f32)
        total, c_far, c_near = lax.optimization_barrier((total, c_far, c_near))
        total = total[:, : 2 * width] + swap_t(total[:, 2 * width :].astype(bf16), 1, decoders).astype(f32)
        total = total.astype(bf16)
        return fwd_shard, fwd_shard[:part], jnp.concatenate([c_near, c_near], axis=1), c_far, dn, total

    enc_y, top, near, c_far, dn, total = lax.cond(~dec, enc_phase1, dec_phase1, 0)

    arrivals = [
        move(total, lambda y, x, z, c, tt: (1, x, z, c, tt) if y == y_from else None) for y_from in (2, 3)
    ]
    dc_from2, dc_from3 = arrivals
    arrivals = [
        move(top, lambda y, x, z, c, tt: (y_to, x, z_to, c, tt) if y == 1 and z == 1 else None)
        for y_to in (2, 3)
        for z_to in (0, 1)
    ]
    top = sum(arrivals)

    def enc_phase2(_):
        b_full = jnp.concatenate([b_three, near[:, :width]], axis=1)
        first_row = lambda y, z: y == 1
        pair = dc_from2.astype(f32) + dc_from3.astype(f32)
        mine = pair[:, :width] + swap_t(pair[:, width:].astype(bf16), 2, first_row).astype(f32)
        mine16 = mine.astype(bf16)
        mine = mine + move(
            mine16, lambda y, x, z, c, tt: (y, x, 1, c, tt) if y == 1 and z == 0 else None
        ).astype(f32)
        mine = mine.astype(bf16)
        pair = jnp.concatenate([mine, swap_t(mine, 2, top_row)], axis=1)
        u = jnp.concatenate([pair, swap_t(pair, 1, top_row)], axis=1)
        c_pair = jnp.concatenate([cot_shard, c_far], axis=1)
        c_pair, u = tie(c_pair, u)
        c_near = swap_t(c_pair, 1, encoders)
        u = final * u.astype(f32)
        r = inverse_rms(saved)
        block = (r * u - saved * r**3 * jnp.mean(u * saved, axis=-1, keepdims=True)).astype(bf16)
        slots = [block]
        for k in range(1, NX):
            slots.append(
                move(block, lambda y, x, z, c, tt: (y, NX - 1, z, c, tt) if top_row(y, z) and x ^ k == NX - 1 else None)
            )
        slots = jnp.concatenate(slots, axis=0)
        slots, c_near = tie(slots, c_near)
        c_full = jnp.concatenate([c_pair, c_near], axis=1)
        swapped = swap_core(slots, top_row)
        pieces = []
        for xi in range(NX):
            k = xi ^ (NX - 1)
            pieces += [swapped[k * part : (k + 1) * part], slots[k * part : (k + 1) * part]]
        returned_full = jnp.concatenate(pieces, axis=0)
        sent = move(enc_y, following(False))
        values = b_full.astype(f32)
        inverse = inverse_rms(values)
        normed = scale_rows(values, inverse, gain)
        q, k, v = project(normed, normed)
        upstream = jnp.where(last, returned_full, c_full)
        dq, dk, dv = attend_back(q, k, v, upstream, w_o)
        term = (mm_t(dq, w_q) + mm_t(dk, w_k) + mm_t(dv, w_v)).astype(bf16)
        term, sent = tie(term, sent)
        summed, row_sum, _ = scatter(term, jnp.sum(gain * term.astype(f32) * values, axis=-1), encoders)
        return sent, summed, row_sum, inverse, upstream[:, :width]

    def dec_phase2(_):
        all_top = jnp.concatenate([top, swap_t(top, 2, decoders)], axis=1)
        all_top = jnp.concatenate([all_top, swap_t(all_top, 1, decoders)], axis=1).astype(f32)
        row_part = jnp.sum(gain * dn.astype(f32) * a_values, axis=-1)
        dn_tied, all_top, c_last = lax.optimization_barrier((dn, all_top, c_far))
        c_last = swap_t(c_last, 1, decoders)
        c_full = jnp.concatenate([fwd_shard, c_far, near[:, :width], c_last], axis=1)
        dn_pair, row_part = scatter_near(dn_tied, row_part, decoders)
        top_full = gather_rows(scale_rows(all_top, inverse_rms(all_top), final), decoders)
        values = c_full.astype(f32)
        normed = scale_rows(values, inverse_rms(values), gain)
        out = attend_out(*project(normed, top_full), w_o).astype(bf16)
        dn_sum, row_sum, out = scatter_far(dn_pair, row_part, decoders, out)
        summed, _, dn_sum = scatter(out, None, decoders, dn_sum)
        dec_y = (fwd_shard.astype(f32) + summed).astype(bf16)
        return dec_y, dn_sum, row_sum, a_inverse, cot_shard

    sent, summed, row_sum, inverse, upstream = lax.cond(dec, dec_phase2, enc_phase2, 0)
    arrived = move(sent, following(True))
    from_enc = (~dec) & (section_index > 0)
    fwd_out = jnp.where(from_enc, sent, arrived)[None]
    grad_in = (
        upstream.astype(f32)
        + inverse * (gain[:, :width] * summed)
        - bwd_shard.astype(f32) * inverse**3 * (row_sum / full)
    ).astype(bf16)[None]
    return (fwd_out, grad_in)


def solution(mesh):
    in_specs = (
        P("section", None, "tensor"),
        P("section", None, "tensor"),
        P("section", None, "tensor"),
        P(None, "tensor"),
        P("section", "tensor"),
        P("tensor"),
        P("section", None, None, "tensor"),
        P("section", "tensor", None),
    )
    out_specs = (P("section", None, "tensor"), P("section", None, "tensor"))
    return jax.shard_map(body, mesh=mesh, in_specs=in_specs, out_specs=out_specs, check_vma=False)
```

```python
import jax
import jax.numpy as jnp
from jax import lax
from jax.sharding import PartitionSpec as P

HEAD_DIM = 256
NY, NX, NZ, NC, NT = 4, 4, 2, 2, 4
SECTION_COUNT = NY * NX * NZ * NC
ENC_SECTIONS = SECTION_COUNT // 2
LAST = ENC_SECTIONS - 1

epsilon = 1e-06
f32 = jnp.float32
bf16 = jnp.bfloat16

PLACES = [
    (y, x, z, c, t)
    for y in range(NY)
    for x in range(NX)
    for z in range(NZ)
    for c in range(NC)
    for t in range(NT)
]


def place_index(place):
    y, x, z, c, t = place
    return (((y * NX + x) * NZ + z) * NC + c) * NT + t


def section_of(place):
    return place_index(place) // NT


def move(value, route):
    pairs = []
    for place in PLACES:
        target = route(*place)
        if target is not None:
            pairs.append((place_index(place), place_index(target)))
    return lax.ppermute(value, ("section", "tensor"), pairs)


def is_dec(y):
    return y >= NY // 2


def everyone(y, z):
    return True


def encoders(y, z):
    return y < NY // 2


def decoders(y, z):
    return y >= NY // 2


def top_row(y, z):
    return y == 1 and z == 1


def swap_x(value, k, who):
    return move(value, lambda y, x, z, c, t: (y, x ^ k, z, c, t) if who(y, z) else None)


def swap_core(value, who):
    return move(value, lambda y, x, z, c, t: (y, x, z, 1 - c, t) if who(y, z) else None)


def swap_t(value, k, who):
    return move(value, lambda y, x, z, c, t: (y, x, z, c, t ^ k) if who(y, z) else None)


def after(value, *others):
    return lax.optimization_barrier((value,) + others)[0]


def tie(value, other):
    return lax.optimization_barrier((value, other))


def high_low(row_part, columns):
    high = row_part.astype(bf16)
    both = jnp.concatenate([high, (row_part - high.astype(f32)).astype(bf16)])
    spare = -both.shape[0] % columns
    return jnp.pad(both, (0, spare)).reshape(-1, columns)


def scatter_near(total, row_part, who):
    rows, half = total.shape[0], total.shape[1] // 2
    give = total[:, half:]
    if row_part is not None:
        give = jnp.concatenate([give, high_low(row_part, half)], axis=0)
    got = swap_t(give, 1, who).astype(f32)
    pair = total[:, :half].astype(f32) + got[:rows]
    if row_part is None:
        return pair, None
    tail = got[rows:].reshape(-1)
    return pair, row_part + tail[:rows] + tail[rows : 2 * rows]


def scatter_far(pair, sums, who, beside=None):
    rows, width = pair.shape[0], pair.shape[1] // 2
    give = pair[:, width:].astype(bf16)
    if sums is not None:
        give = jnp.concatenate([give, high_low(sums, width)], axis=0)
    if beside is not None:
        give, beside = tie(give, beside)
    got = swap_t(give, 2, who).astype(f32)
    summed = pair[:, :width] + got[:rows]
    if sums is not None:
        tail = got[rows:].reshape(-1)
        sums = (sums + tail[:rows] + tail[rows : 2 * rows]).reshape(rows, 1)
    return summed, sums, beside


def scatter(total, row_part, who, beside=None):
    rows, width = total.shape[0], total.shape[1] // NT
    give3 = total[:, 3 * width :]
    if row_part is not None:
        give3 = jnp.concatenate([give3, high_low(row_part, width)], axis=0)
    give1, got3 = tie(total[:, 2 * width : 3 * width], swap_t(give3, 1, who))
    got3 = got3.astype(f32)
    give2 = (total[:, width : 2 * width].astype(f32) + got3[:rows]).astype(bf16)
    if row_part is not None:
        tail = got3[rows:].reshape(-1)
        row_part = row_part + tail[:rows] + tail[rows : 2 * rows]
        give2 = jnp.concatenate([give2, high_low(row_part, width)], axis=0)
    if beside is not None:
        give2, beside = tie(give2, beside)
    got2 = swap_t(give2, 2, who).astype(f32)
    got1 = swap_t(give1, 1, who).astype(f32)
    summed = total[:, :width].astype(f32) + got1 + got2[:rows]
    if row_part is not None:
        tail = got2[rows:].reshape(-1)
        row_part = (row_part + tail[:rows] + tail[rows : 2 * rows]).reshape(rows, 1)
    return summed, row_part, beside


def inverse_rms(values):
    return lax.rsqrt(jnp.mean(values * values, axis=-1, keepdims=True) + epsilon)


def scale_rows(values, inverse, gain_row):
    return (values * inverse * gain_row).astype(bf16)


def mm(a, b):
    return jnp.dot(a, b, preferred_element_type=f32)


def mm_t(a, b):
    return lax.dot_general(a, b, (((1,), (1,)), ((), ())), preferred_element_type=f32)


def t_mm(a, b):
    return lax.dot_general(a, b, (((0,), (0,)), ((), ())), preferred_element_type=f32)


def heads_of(matrix):
    return [matrix[:, h * HEAD_DIM : (h + 1) * HEAD_DIM] for h in range(matrix.shape[1] // HEAD_DIM)]


def softmax_rows(queries, keys):
    weights = jnp.exp(mm_t(queries, keys) * HEAD_DIM ** (-0.5))
    return weights / jnp.sum(weights, axis=-1, keepdims=True)


def attend_out(q, k, v, w_proj):
    mixed = [
        mm(softmax_rows(qh, kh).astype(bf16), vh).astype(bf16)
        for qh, kh, vh in zip(heads_of(q), heads_of(k), heads_of(v))
    ]
    return mm(jnp.concatenate(mixed, axis=1), w_proj)


def attend_back(q, k, v, upstream, w_proj):
    grad_mix = mm_t(upstream, w_proj).astype(bf16)
    dq, dk, dv = [], [], []
    for qh, kh, vh, gh in zip(heads_of(q), heads_of(k), heads_of(v), heads_of(grad_mix)):
        weights = softmax_rows(qh, kh)
        dv.append(t_mm(weights.astype(bf16), gh).astype(bf16))
        grad_weights = mm_t(gh, vh)
        grad_scores = (
            weights
            * (grad_weights - jnp.sum(weights * grad_weights, axis=-1, keepdims=True))
            * HEAD_DIM ** (-0.5)
        ).astype(bf16)
        dq.append(mm(grad_scores, kh).astype(bf16))
        dk.append(t_mm(grad_scores, qh).astype(bf16))
    return [jnp.concatenate(parts, axis=1) for parts in (dq, dk, dv)]


def gather_rows(own, who):
    half = jnp.concatenate([own] + [swap_x(own, k, who) for k in range(1, NX)], axis=0)
    return jnp.concatenate([half, swap_core(half, who)], axis=0)


def following(kind):
    def go(y, x, z, c, t):
        s = section_of((y, x, z, c, t))
        n = ((s + 1) % SECTION_COUNT) * NT + t
        return None if s == LAST or is_dec(y) != kind else PLACES[n]

    return go


def body(fwd_in, bwd_in, cotangent, enc_saved, norm_gain, final_gain, w_qkv, w_out):
    section_index = lax.axis_index("section")
    t = lax.axis_index("tensor")
    core = section_index % NC
    x_at = section_index // (NC * NZ) % NX
    dec = section_index >= ENC_SECTIONS
    last = section_index == LAST
    fwd_shard, bwd_shard, cot_shard = fwd_in[0], bwd_in[0], cotangent[0]
    rows, width = fwd_shard.shape
    full = width * NT
    part = rows // (NX * NC)
    half = rows // NC

    own_rows = lax.dynamic_slice_in_dim(enc_saved, (x_at * NC + core) * part, part, 0)
    a_shard = jnp.concatenate(
        [jnp.where(dec, bwd_shard, fwd_shard), own_rows, norm_gain, final_gain[None]], axis=0
    )
    b_shard = jnp.where(dec, cot_shard, bwd_shard)
    a_far = swap_t(a_shard, 2, everyone)
    a_near = swap_t(a_shard, 1, everyone)
    a_last = swap_t(a_far, 1, everyone)
    b_far = swap_t(after(b_shard, a_far), 2, everyone)
    b_own, a_near = tie(b_shard, a_near)
    b_near = swap_t(b_own, 1, everyone)
    a_all = jnp.concatenate([a_shard, a_far, a_near, a_last], axis=1)
    b_three = jnp.concatenate([b_shard, b_far, b_near], axis=1)

    small = a_all[rows:].astype(f32)
    saved, gain, final = small[:part], small[part : part + 1], small[part + 1 :]

    order = [t, t ^ 2, t ^ 1, t ^ 3]
    w_in = w_qkv[0]
    turned = [lax.dynamic_slice_in_dim(w_in, o * width, width, 0) for o in order]
    w_q, w_k, w_v = (jnp.concatenate([w[:, i] for w in turned], axis=0) for i in range(3))
    w_o = jnp.concatenate([lax.dynamic_slice_in_dim(w_out[0], o * width, width, 1) for o in order], axis=1)

    def normed_a():
        values = a_all[:rows].astype(f32)
        return scale_rows(values, inverse_rms(values), gain)
    def project(normed, source):
        return mm(normed, w_q).astype(bf16), mm(source, w_k).astype(bf16), mm(source, w_v).astype(bf16)

    def enc_phase1(_):
        b_last = swap_t(b_far, 1, encoders)
        c_far = swap_t(cot_shard, 2, encoders)
        a_normed = normed_a()
        out = attend_out(*project(a_normed, a_normed), w_o).astype(bf16)
        out, b_last = tie(out, b_last)
        summed, _, c_far = scatter(out, None, encoders, c_far)
        enc_y = (fwd_shard.astype(f32) + summed).astype(bf16)
        blocks = enc_y.reshape(NX, NC, part, width)
        blocks = jnp.where(core == 1, blocks[:, 1], swap_core(blocks[:, 0], top_row))
        top = blocks[NX - 1]
        for k in range(1, NX):
            sent = move(
                blocks[(NX - 1) ^ k], lambda y, x, z, c, tt: (y, x ^ k, z, c, tt) if top_row(y, z) and x == NX - 1 else None
            )
            top = jnp.where(x_at ^ (NX - 1) == k, sent, top)
        return enc_y, top, jnp.concatenate([b_last, b_last], axis=1), c_far, out, out[:part, : 2 * width]

    def dec_phase1(_):
        b_last = swap_t(b_far, 1, decoders)
        saved_rows = scale_rows(saved, inverse_rms(saved), final)
        saved_half = jnp.concatenate([saved_rows] + [swap_x(saved_rows, k, decoders) for k in range(1, NX)], axis=0)
        saved_half, b_last = tie(saved_half, b_last)
        saved_normed = jnp.concatenate([saved_half, swap_core(saved_half, decoders)], axis=0)
        q, k, v = project(normed_a(), saved_normed)
        c_shard, b_last = tie(fwd_shard, b_last)
        c_far, c_near = swap_t(c_shard, 2, decoders), swap_t(c_shard, 1, decoders)
        b_full = jnp.concatenate([b_three, b_last], axis=1)
        dq, dk, dv = attend_back(q, k, v, b_full, w_o)
        dc = (mm_t(dk, w_k) + mm_t(dv, w_v)).astype(bf16)
        dn = mm_t(dq, w_q).astype(bf16)
        acc = dc[:half].astype(f32) + swap_core(dc[half:], decoders).astype(f32)
        acc16 = acc.astype(bf16)
        total = acc[:part]
        for k in range(1, NX):
            total = total + swap_x(acc16[k * part : (k + 1) * part], k, decoders).astype(f32)
        total, c_far, c_near = lax.optimization_barrier((total, c_far, c_near))
        total = total[:, : 2 * width] + swap_t(total[:, 2 * width :].astype(bf16), 1, decoders).astype(f32)
        total = total.astype(bf16)
        return fwd_shard, fwd_shard[:part], jnp.concatenate([c_near, c_near], axis=1), c_far, dn, total

    enc_y, top, near, c_far, dn, total = lax.cond(~dec, enc_phase1, dec_phase1, 0)

    arrivals = [
        move(total, lambda y, x, z, c, tt: (1, x, z, c, tt) if y == y_from else None) for y_from in (2, 3)
    ]
    dc_from2, dc_from3 = arrivals
    arrivals = [
        move(top, lambda y, x, z, c, tt: (y_to, x, z_to, c, tt) if y == 1 and z == 1 else None)
        for y_to in (2, 3)
        for z_to in (0, 1)
    ]
    top = sum(arrivals)

    def enc_phase2(_):
        b_full = jnp.concatenate([b_three, near[:, :width]], axis=1)
        first_row = lambda y, z: y == 1
        pair = dc_from2.astype(f32) + dc_from3.astype(f32)
        mine = pair[:, :width] + swap_t(pair[:, width:].astype(bf16), 2, first_row).astype(f32)
        mine16 = mine.astype(bf16)
        mine = mine + move(
            mine16, lambda y, x, z, c, tt: (y, x, 1, c, tt) if y == 1 and z == 0 else None
        ).astype(f32)
        mine = mine.astype(bf16)
        pair = jnp.concatenate([mine, swap_t(mine, 2, top_row)], axis=1)
        u = jnp.concatenate([pair, swap_t(pair, 1, top_row)], axis=1)
        c_pair = jnp.concatenate([cot_shard, c_far], axis=1)
        c_pair, u = tie(c_pair, u)
        c_near = swap_t(c_pair, 1, encoders)
        u = final * u.astype(f32)
        r = inverse_rms(saved)
        block = (r * u - saved * r**3 * jnp.mean(u * saved, axis=-1, keepdims=True)).astype(bf16)
        slots = [block]
        for k in range(1, NX):
            slots.append(
                move(block, lambda y, x, z, c, tt: (y, NX - 1, z, c, tt) if top_row(y, z) and x ^ k == NX - 1 else None)
            )
        slots = jnp.concatenate(slots, axis=0)
        slots, c_near = tie(slots, c_near)
        c_full = jnp.concatenate([c_pair, c_near], axis=1)
        swapped = swap_core(slots, top_row)
        pieces = []
        for xi in range(NX):
            k = xi ^ (NX - 1)
            pieces += [swapped[k * part : (k + 1) * part], slots[k * part : (k + 1) * part]]
        returned_full = jnp.concatenate(pieces, axis=0)
        sent = move(enc_y, following(False))
        values = b_full.astype(f32)
        inverse = inverse_rms(values)
        normed = scale_rows(values, inverse, gain)
        q, k, v = project(normed, normed)
        upstream = jnp.where(last, returned_full, c_full)
        dq, dk, dv = attend_back(q, k, v, upstream, w_o)
        term = (mm_t(dq, w_q) + mm_t(dk, w_k) + mm_t(dv, w_v)).astype(bf16)
        term, sent = tie(term, sent)
        summed, row_sum, _ = scatter(term, jnp.sum(gain * term.astype(f32) * values, axis=-1), encoders)
        return sent, summed, row_sum, inverse, upstream[:, :width]

    def dec_phase2(_):
        all_top = jnp.concatenate([top, swap_t(top, 2, decoders)], axis=1)
        all_top = jnp.concatenate([all_top, swap_t(all_top, 1, decoders)], axis=1).astype(f32)
        a_values = a_all[:rows].astype(f32)
        a_inverse = inverse_rms(a_values)
        row_part = jnp.sum(gain * dn.astype(f32) * a_values, axis=-1)
        dn_tied, all_top, c_last = lax.optimization_barrier((dn, all_top, c_far))
        c_last = swap_t(c_last, 1, decoders)
        c_full = jnp.concatenate([fwd_shard, c_far, near[:, :width], c_last], axis=1)
        dn_pair, row_part = scatter_near(dn_tied, row_part, decoders)
        top_full = gather_rows(scale_rows(all_top, inverse_rms(all_top), final), decoders)
        values = c_full.astype(f32)
        normed = scale_rows(values, inverse_rms(values), gain)
        out = attend_out(*project(normed, top_full), w_o).astype(bf16)
        dn_sum, row_sum, out = scatter_far(dn_pair, row_part, decoders, out)
        summed, _, dn_sum = scatter(out, None, decoders, dn_sum)
        dec_y = (fwd_shard.astype(f32) + summed).astype(bf16)
        return dec_y, dn_sum, row_sum, a_inverse, cot_shard

    sent, summed, row_sum, inverse, upstream = lax.cond(dec, dec_phase2, enc_phase2, 0)
    arrived = move(sent, following(True))
    from_enc = (~dec) & (section_index > 0)
    fwd_out = jnp.where(from_enc, sent, arrived)[None]
    grad_in = (
        upstream.astype(f32)
        + inverse * (gain[:, :width] * summed)
        - bwd_shard.astype(f32) * inverse**3 * (row_sum / full)
    ).astype(bf16)[None]
    return (fwd_out, grad_in)


def solution(mesh):
    in_specs = (
        P("section", None, "tensor"),
        P("section", None, "tensor"),
        P("section", None, "tensor"),
        P(None, "tensor"),
        P("section", "tensor"),
        P("tensor"),
        P("section", None, None, "tensor"),
        P("section", "tensor", None),
    )
    out_specs = (P("section", None, "tensor"), P("section", None, "tensor"))
    return jax.shard_map(body, mesh=mesh, in_specs=in_specs, out_specs=out_specs, check_vma=False)
```

```python
import jax
import jax.numpy as jnp
from jax import lax
from jax.sharding import PartitionSpec as P

HEAD_DIM = 256
NY, NX, NZ, NC, NT = 4, 4, 2, 2, 4
SECTION_COUNT = NY * NX * NZ * NC
ENC_SECTIONS = SECTION_COUNT // 2
LAST = ENC_SECTIONS - 1

epsilon = 1e-06
f32 = jnp.float32
bf16 = jnp.bfloat16

PLACES = [
    (y, x, z, c, t)
    for y in range(NY)
    for x in range(NX)
    for z in range(NZ)
    for c in range(NC)
    for t in range(NT)
]


def place_index(place):
    y, x, z, c, t = place
    return (((y * NX + x) * NZ + z) * NC + c) * NT + t


def section_of(place):
    return place_index(place) // NT


def move(value, route):
    pairs = []
    for place in PLACES:
        target = route(*place)
        if target is not None:
            pairs.append((place_index(place), place_index(target)))
    return lax.ppermute(value, ("section", "tensor"), pairs)


def is_dec(y):
    return y >= NY // 2


def everyone(y, z):
    return True


def encoders(y, z):
    return y < NY // 2


def decoders(y, z):
    return y >= NY // 2


def top_row(y, z):
    return y == 1 and z == 1


def swap_x(value, k, who):
    return move(value, lambda y, x, z, c, t: (y, x ^ k, z, c, t) if who(y, z) else None)


def swap_core(value, who):
    return move(value, lambda y, x, z, c, t: (y, x, z, 1 - c, t) if who(y, z) else None)


def swap_t(value, k, who):
    return move(value, lambda y, x, z, c, t: (y, x, z, c, t ^ k) if who(y, z) else None)


def after(value, *others):
    return lax.optimization_barrier((value,) + others)[0]


def tie(value, other):
    return lax.optimization_barrier((value, other))


def high_low(row_part, columns):
    high = row_part.astype(bf16)
    both = jnp.concatenate([high, (row_part - high.astype(f32)).astype(bf16)])
    spare = -both.shape[0] % columns
    return jnp.pad(both, (0, spare)).reshape(-1, columns)


def scatter_near(total, row_part, who):
    rows, half = total.shape[0], total.shape[1] // 2
    give = total[:, half:]
    if row_part is not None:
        give = jnp.concatenate([give, high_low(row_part, half)], axis=0)
    got = swap_t(give, 1, who).astype(f32)
    pair = total[:, :half].astype(f32) + got[:rows]
    if row_part is None:
        return pair, None
    tail = got[rows:].reshape(-1)
    return pair, row_part + tail[:rows] + tail[rows : 2 * rows]


def scatter_far(pair, sums, who, beside=None):
    rows, width = pair.shape[0], pair.shape[1] // 2
    give = pair[:, width:].astype(bf16)
    if sums is not None:
        give = jnp.concatenate([give, high_low(sums, width)], axis=0)
    if beside is not None:
        give, beside = tie(give, beside)
    got = swap_t(give, 2, who).astype(f32)
    summed = pair[:, :width] + got[:rows]
    if sums is not None:
        tail = got[rows:].reshape(-1)
        sums = (sums + tail[:rows] + tail[rows : 2 * rows]).reshape(rows, 1)
    return summed, sums, beside


def scatter(total, row_part, who, beside=None):
    rows, width = total.shape[0], total.shape[1] // NT
    give3 = total[:, 3 * width :]
    if row_part is not None:
        give3 = jnp.concatenate([give3, high_low(row_part, width)], axis=0)
    give1, got3 = tie(total[:, 2 * width : 3 * width], swap_t(give3, 1, who))
    got3 = got3.astype(f32)
    give2 = (total[:, width : 2 * width].astype(f32) + got3[:rows]).astype(bf16)
    if row_part is not None:
        tail = got3[rows:].reshape(-1)
        row_part = row_part + tail[:rows] + tail[rows : 2 * rows]
        give2 = jnp.concatenate([give2, high_low(row_part, width)], axis=0)
    if beside is not None:
        give2, beside = tie(give2, beside)
    got2 = swap_t(give2, 2, who).astype(f32)
    got1 = swap_t(give1, 1, who).astype(f32)
    summed = total[:, :width].astype(f32) + got1 + got2[:rows]
    if row_part is not None:
        tail = got2[rows:].reshape(-1)
        row_part = (row_part + tail[:rows] + tail[rows : 2 * rows]).reshape(rows, 1)
    return summed, row_part, beside


def inverse_rms(values):
    return lax.rsqrt(jnp.mean(values * values, axis=-1, keepdims=True) + epsilon)


def scale_rows(values, inverse, gain_row):
    return (values * inverse * gain_row).astype(bf16)


def mm(a, b):
    return jnp.dot(a, b, preferred_element_type=f32)


def mm_t(a, b):
    return lax.dot_general(a, b, (((1,), (1,)), ((), ())), preferred_element_type=f32)


def t_mm(a, b):
    return lax.dot_general(a, b, (((0,), (0,)), ((), ())), preferred_element_type=f32)


def heads_of(matrix):
    return [matrix[:, h * HEAD_DIM : (h + 1) * HEAD_DIM] for h in range(matrix.shape[1] // HEAD_DIM)]


def softmax_rows(queries, keys):
    weights = jnp.exp(mm_t(queries, keys) * HEAD_DIM ** (-0.5))
    return weights / jnp.sum(weights, axis=-1, keepdims=True)


def attend_out(q, k, v, w_proj):
    mixed = [
        mm(softmax_rows(qh, kh).astype(bf16), vh).astype(bf16)
        for qh, kh, vh in zip(heads_of(q), heads_of(k), heads_of(v))
    ]
    return mm(jnp.concatenate(mixed, axis=1), w_proj)


def attend_back(q, k, v, upstream, w_proj):
    grad_mix = mm_t(upstream, w_proj).astype(bf16)
    dq, dk, dv = [], [], []
    for qh, kh, vh, gh in zip(heads_of(q), heads_of(k), heads_of(v), heads_of(grad_mix)):
        weights = softmax_rows(qh, kh)
        dv.append(t_mm(weights.astype(bf16), gh).astype(bf16))
        grad_weights = mm_t(gh, vh)
        grad_scores = (
            weights
            * (grad_weights - jnp.sum(weights * grad_weights, axis=-1, keepdims=True))
            * HEAD_DIM ** (-0.5)
        ).astype(bf16)
        dq.append(mm(grad_scores, kh).astype(bf16))
        dk.append(t_mm(grad_scores, qh).astype(bf16))
    return [jnp.concatenate(parts, axis=1) for parts in (dq, dk, dv)]


def gather_rows(own, who):
    half = jnp.concatenate([own] + [swap_x(own, k, who) for k in range(1, NX)], axis=0)
    return jnp.concatenate([half, swap_core(half, who)], axis=0)


def following(kind):
    def go(y, x, z, c, t):
        s = section_of((y, x, z, c, t))
        n = ((s + 1) % SECTION_COUNT) * NT + t
        return None if s == LAST or is_dec(y) != kind else PLACES[n]

    return go


def body(fwd_in, bwd_in, cotangent, enc_saved, norm_gain, final_gain, w_qkv, w_out):
    section_index = lax.axis_index("section")
    t = lax.axis_index("tensor")
    core = section_index % NC
    x_at = section_index // (NC * NZ) % NX
    dec = section_index >= ENC_SECTIONS
    last = section_index == LAST
    fwd_shard, bwd_shard, cot_shard = fwd_in[0], bwd_in[0], cotangent[0]
    rows, width = fwd_shard.shape
    full = width * NT
    part = rows // (NX * NC)
    half = rows // NC

    own_rows = lax.dynamic_slice_in_dim(enc_saved, (x_at * NC + core) * part, part, 0)
    a_shard = jnp.concatenate(
        [jnp.where(dec, bwd_shard, fwd_shard), own_rows, norm_gain, final_gain[None]], axis=0
    )
    b_shard = jnp.where(dec, cot_shard, bwd_shard)
    a_far = swap_t(a_shard, 2, everyone)
    a_near = swap_t(a_shard, 1, everyone)
    a_last = swap_t(a_far, 1, everyone)
    b_far = swap_t(after(b_shard, a_far), 2, everyone)
    b_own, a_near = tie(b_shard, a_near)
    b_near = swap_t(b_own, 1, everyone)
    a_all = jnp.concatenate([a_shard, a_far, a_near, a_last], axis=1)
    b_three = jnp.concatenate([b_shard, b_far, b_near], axis=1)

    small = a_all[rows:].astype(f32)
    saved, gain, final = small[:part], small[part : part + 1], small[part + 1 :]

    order = [t, t ^ 2, t ^ 1, t ^ 3]
    w_in = w_qkv[0]
    turned = [lax.dynamic_slice_in_dim(w_in, o * width, width, 0) for o in order]
    w_q, w_k, w_v = (jnp.concatenate([w[:, i] for w in turned], axis=0) for i in range(3))
    w_o = jnp.concatenate([lax.dynamic_slice_in_dim(w_out[0], o * width, width, 1) for o in order], axis=1)

    def normed_a():
        values = a_all[:rows].astype(f32)
        return scale_rows(values, inverse_rms(values), gain)
    def project(normed, source):
        return mm(normed, w_q).astype(bf16), mm(source, w_k).astype(bf16), mm(source, w_v).astype(bf16)

    def enc_phase1(_):
        b_last = swap_t(b_far, 1, encoders)
        c_far = swap_t(cot_shard, 2, encoders)
        a_normed = normed_a()
        out = attend_out(*project(a_normed, a_normed), w_o).astype(bf16)
        out, b_last, c_far = lax.optimization_barrier((out, b_last, c_far))
        summed, _, _ = scatter(out, None, encoders)
        enc_y = (fwd_shard.astype(f32) + summed).astype(bf16)
        blocks = enc_y.reshape(NX, NC, part, width)
        blocks = jnp.where(core == 1, blocks[:, 1], swap_core(blocks[:, 0], top_row))
        top = blocks[NX - 1]
        for k in range(1, NX):
            sent = move(
                blocks[(NX - 1) ^ k], lambda y, x, z, c, tt: (y, x ^ k, z, c, tt) if top_row(y, z) and x == NX - 1 else None
            )
            top = jnp.where(x_at ^ (NX - 1) == k, sent, top)
        return enc_y, top, jnp.concatenate([b_last, b_last], axis=1), c_far, out, out[:part, : 2 * width]

    def dec_phase1(_):
        b_last = swap_t(b_far, 1, decoders)
        saved_rows = scale_rows(saved, inverse_rms(saved), final)
        saved_half = jnp.concatenate([saved_rows] + [swap_x(saved_rows, k, decoders) for k in range(1, NX)], axis=0)
        saved_half, b_last = tie(saved_half, b_last)
        saved_normed = jnp.concatenate([saved_half, swap_core(saved_half, decoders)], axis=0)
        q, k, v = project(normed_a(), saved_normed)
        c_shard, b_last = tie(fwd_shard, b_last)
        c_far, c_near = swap_t(c_shard, 2, decoders), swap_t(c_shard, 1, decoders)
        b_full = jnp.concatenate([b_three, b_last], axis=1)
        dq, dk, dv = attend_back(q, k, v, b_full, w_o)
        dc = (mm_t(dk, w_k) + mm_t(dv, w_v)).astype(bf16)
        dn = mm_t(dq, w_q).astype(bf16)
        acc = dc[:half].astype(f32) + swap_core(dc[half:], decoders).astype(f32)
        acc16 = acc.astype(bf16)
        total = acc[:part]
        for k in range(1, NX):
            total = total + swap_x(acc16[k * part : (k + 1) * part], k, decoders).astype(f32)
        total, c_far, c_near = lax.optimization_barrier((total, c_far, c_near))
        total = total[:, : 2 * width] + swap_t(total[:, 2 * width :].astype(bf16), 1, decoders).astype(f32)
        total = total.astype(bf16)
        return fwd_shard, fwd_shard[:part], jnp.concatenate([c_near, c_near], axis=1), c_far, dn, total

    enc_y, top, near, c_far, dn, total = lax.cond(~dec, enc_phase1, dec_phase1, 0)

    arrivals = [
        move(total, lambda y, x, z, c, tt: (1, x, z, c, tt) if y == y_from else None) for y_from in (2, 3)
    ]
    dc_from2, dc_from3 = arrivals
    arrivals = [
        move(top, lambda y, x, z, c, tt: (y_to, x, z_to, c, tt) if y == 1 and z == 1 else None)
        for y_to in (2, 3)
        for z_to in (0, 1)
    ]
    top = sum(arrivals)

    def enc_phase2(_):
        b_full = jnp.concatenate([b_three, near[:, :width]], axis=1)
        first_row = lambda y, z: y == 1
        pair = dc_from2.astype(f32) + dc_from3.astype(f32)
        mine = pair[:, :width] + swap_t(pair[:, width:].astype(bf16), 2, first_row).astype(f32)
        mine16 = mine.astype(bf16)
        mine = mine + move(
            mine16, lambda y, x, z, c, tt: (y, x, 1, c, tt) if y == 1 and z == 0 else None
        ).astype(f32)
        mine = mine.astype(bf16)
        pair = jnp.concatenate([mine, swap_t(mine, 2, top_row)], axis=1)
        u = jnp.concatenate([pair, swap_t(pair, 1, top_row)], axis=1)
        c_pair = jnp.concatenate([cot_shard, c_far], axis=1)
        c_pair, u = tie(c_pair, u)
        c_near = swap_t(c_pair, 1, encoders)
        u = final * u.astype(f32)
        r = inverse_rms(saved)
        block = (r * u - saved * r**3 * jnp.mean(u * saved, axis=-1, keepdims=True)).astype(bf16)
        slots = [block]
        for k in range(1, NX):
            slots.append(
                move(block, lambda y, x, z, c, tt: (y, NX - 1, z, c, tt) if top_row(y, z) and x ^ k == NX - 1 else None)
            )
        slots = jnp.concatenate(slots, axis=0)
        slots, c_near = tie(slots, c_near)
        c_full = jnp.concatenate([c_pair, c_near], axis=1)
        swapped = swap_core(slots, top_row)
        pieces = []
        for xi in range(NX):
            k = xi ^ (NX - 1)
            pieces += [swapped[k * part : (k + 1) * part], slots[k * part : (k + 1) * part]]
        returned_full = jnp.concatenate(pieces, axis=0)
        sent = move(enc_y, following(False))
        values = b_full.astype(f32)
        inverse = inverse_rms(values)
        normed = scale_rows(values, inverse, gain)
        q, k, v = project(normed, normed)
        upstream = jnp.where(last, returned_full, c_full)
        dq, dk, dv = attend_back(q, k, v, upstream, w_o)
        term = (mm_t(dq, w_q) + mm_t(dk, w_k) + mm_t(dv, w_v)).astype(bf16)
        term, sent = tie(term, sent)
        summed, row_sum, _ = scatter(term, jnp.sum(gain * term.astype(f32) * values, axis=-1), encoders)
        return sent, summed, row_sum, inverse, upstream[:, :width]

    def dec_phase2(_):
        all_top = jnp.concatenate([top, swap_t(top, 2, decoders)], axis=1)
        all_top = jnp.concatenate([all_top, swap_t(all_top, 1, decoders)], axis=1).astype(f32)
        a_values = a_all[:rows].astype(f32)
        a_inverse = inverse_rms(a_values)
        row_part = jnp.sum(gain * dn.astype(f32) * a_values, axis=-1)
        dn_tied, all_top, c_last = lax.optimization_barrier((dn, all_top, c_far))
        c_last = swap_t(c_last, 1, decoders)
        c_full = jnp.concatenate([fwd_shard, c_far, near[:, :width], c_last], axis=1)
        dn_pair, row_part = scatter_near(dn_tied, row_part, decoders)
        top_full = gather_rows(scale_rows(all_top, inverse_rms(all_top), final), decoders)
        values = c_full.astype(f32)
        normed = scale_rows(values, inverse_rms(values), gain)
        out = attend_out(*project(normed, top_full), w_o).astype(bf16)
        dn_sum, row_sum, out = scatter_far(dn_pair, row_part, decoders, out)
        summed, _, dn_sum = scatter(out, None, decoders, dn_sum)
        dec_y = (fwd_shard.astype(f32) + summed).astype(bf16)
        return dec_y, dn_sum, row_sum, a_inverse, cot_shard

    sent, summed, row_sum, inverse, upstream = lax.cond(dec, dec_phase2, enc_phase2, 0)
    arrived = move(sent, following(True))
    from_enc = (~dec) & (section_index > 0)
    fwd_out = jnp.where(from_enc, sent, arrived)[None]
    grad_in = (
        upstream.astype(f32)
        + inverse * (gain[:, :width] * summed)
        - bwd_shard.astype(f32) * inverse**3 * (row_sum / full)
    ).astype(bf16)[None]
    return (fwd_out, grad_in)


def solution(mesh):
    in_specs = (
        P("section", None, "tensor"),
        P("section", None, "tensor"),
        P("section", None, "tensor"),
        P(None, "tensor"),
        P("section", "tensor"),
        P("tensor"),
        P("section", None, None, "tensor"),
        P("section", "tensor", None),
    )
    out_specs = (P("section", None, "tensor"), P("section", None, "tensor"))
    return jax.shard_map(body, mesh=mesh, in_specs=in_specs, out_specs=out_specs, check_vma=False)
```
